128 devices in a mesh: rcv: 8 (over z, core), shot: 16 (over x, y).
Axes of the slice: x: 4, y: 4, z: 4, core: 2. Of those that a mesh axis runs over, the one named last changes fastest.
Arguments:
- data: bfloat16 [4, 4096, 4096], P(None, 'rcv', 'shot'), may hold values from -6 to 6
- traces: float32 [65536, 2048], P(('rcv', 'shot')), may hold values from -6 to 6
- weight: float32 [65536], P(('rcv', 'shot')), may hold values from 0.5 to 2
- dest: int32 [65536, 1], P(('rcv', 'shot')), may hold values from 0 to 127; in each aligned block of 512 rows (0 to 511, 512 to 1023, ...) at most 8 rows name the same one
- bins: int32 [65536], P(('rcv', 'shot')), may hold values from 0 to 131071
Outputs:
- binned: bfloat16 [4, 4096, 4096], P(None, 'rcv', 'shot')
- multiples: float32 [4, 4096, 4096], P(None, 'rcv', 'shot')
The draws below stay inside these ranges and needn't reach their ends.
Inputs may be any that keep to these rules, and one draw needn't show every extreme that they name: `dest`: among the 512 traces of one device no owner is named more than 8 times; some owner is named exactly 8 times.
All inputs are finite; a program needn't handle non-finite values.
Results may differ from the reference program's by a relative error of at most 0.0014.
Values may be sent and summed in bfloat16 or wider, within the bound.
A program may use at most 320 MiB of HBM per device.

```python
import math
import jax
import jax.numpy as jnp
import numpy as np
from jax import lax

SHOT_DEV = 256
NN = 4096
REC_DEV = 512
NT = 2048
TR_DEV = 512
TRACES = 65536
CAP = 8
STEPS = 4
N_SHOT = 16
DEVICES = 128


def set_ends(entries, key, smallest, largest):
    shape = entries.shape
    index_at = [jax.random.randint(jax.random.fold_in(key, axis), (), 0, shape[axis]) for axis in range(len(shape))]
    entries = entries.at[tuple(index_at)].set(smallest)
    longest = shape.index(max(shape))
    index_at[longest] = (index_at[longest] + 1) % shape[longest]
    return entries.at[tuple(index_at)].set(largest)


def block_levels(stream_key, shape, split, low, largest):
    def one(axis_at, parts):
        draws = jax.random.uniform(jax.random.fold_in(jax.random.fold_in(stream_key, 6), axis_at), (parts,), jnp.float32, low / len(split), largest / len(split))
        return jnp.repeat(jnp.exp(draws), shape[axis_at] // parts).reshape((-1,) + (1,) * (len(shape) - axis_at - 1))

    loudness = one(*split[0])
    for cut in split[1:]:
        loudness = loudness * one(*cut)
    return loudness


def assign_block(rng, own, number, rows, count, top, most, skew):
    ranking = jax.random.permutation(rng, count)
    crowded, common = portions_of(count, rows * top, most, skew, True), portions_of(count, rows * top, most, skew, False)
    places = jnp.arange(count)

    def named(sizes, offset_by):
        used = int((sizes > 0).sum())
        fixed = max(1, used // 4)
        passed = fixed + (places - fixed + offset_by * (used - fixed)) % max(1, count - fixed)
        return jnp.zeros((count,), jnp.int32).at[ranking[jnp.where(places < fixed, places, passed)]].set(jnp.asarray(sizes, jnp.int32))

    sizes = jnp.where(number % 4 == 0, named(crowded, number // 4), named(common, number - number // 4 - 1))
    mixed = jax.random.permutation(jax.random.fold_in(own, 3), count)
    donor, sink = mixed[0:count // 2 * 2:2], mixed[1:count // 2 * 2:2]
    room = jnp.minimum(sizes[donor] - 1, most - sizes[sink]) // 2
    room = jnp.where((donor == ranking[0]) | (sink == ranking[0]) | (sizes[sink] == 0), 0, jnp.maximum(room, 0))
    passed = jax.random.randint(jax.random.fold_in(own, 4), (count // 2,), 0, 1 << 20) % (room + 1)
    sizes = sizes.at[donor].add(-passed).at[sink].add(passed)
    items = jnp.searchsorted(jnp.cumsum(sizes), jnp.arange(rows * top), side="right").astype(jnp.int32)
    listing = items.reshape(top, rows).T
    listing = listing[jax.random.permutation(jax.random.fold_in(own, 1), rows)]
    offset_by = jax.random.randint(jax.random.fold_in(own, 2), (rows, 1), 0, top)
    return jnp.take_along_axis(listing, (jnp.arange(top)[None, :] + offset_by) % top, axis=1)


def portions_of(number_of, total, bound, lean, full):
    loads = [(1 << 20) // math.isqrt(rank ** lean) + 1 for rank in range(1, number_of + 1)]
    largest = bound if full else min(bound, max(-(-total // number_of), total * loads[0] // sum(loads)))
    least = 1 if total - largest >= number_of - 1 else 0
    holding, rest = [largest] + [least] * (number_of - 1), total - largest - least * (number_of - 1)
    while rest > 0:
        free = [i for i in range(1, number_of) if holding[i] < largest] or [i for i in range(1, number_of) if holding[i] < bound]
        pool, remaining = sum([loads[i] for i in free]), rest
        for i in free:
            addition = min(bound - holding[i], max(1, remaining * loads[i] // pool), rest)
            holding[i] = holding[i] + addition
            rest = rest - addition
    return np.array(holding)


def gaussian(own_key, extent, scale, limit, cuts=(), kind=jnp.bfloat16):
    entries = jax.random.normal(own_key, extent, jnp.float32) * scale
    if len(cuts) > 0:
        entries = block_levels(own_key, extent, cuts, -0.22, 0.18) * entries
    return jnp.clip(entries, min=-limit, max=limit).astype(kind)


def setup_inputs(seed: int = 0) -> dict:
    splits = jax.random.split(jax.random.key(seed), 6)
    data = gaussian(splits[0], (4, NN, NN), 1.0, 6.0, ((1, 8), (2, 16)))
    traces = gaussian(splits[1], (TRACES, NT), 1.0, 6.0, ((0, 128),), jnp.float32)
    weight = jnp.clip(jnp.exp(math.log(2.0) - 1.3862944 * jax.random.uniform(splits[2], (TRACES,), jnp.float32) ** block_levels(splits[2], (TRACES,), ((0, 128),), -0.2, 0.2)), 0.5, 2.0)
    dest_keys = jax.random.split(jax.random.fold_in(splits[3], 1), TRACES // TR_DEV)
    dest_turns = jax.random.permutation(jax.random.fold_in(splits[3], 3), TRACES // TR_DEV)
    dest = jax.vmap(lambda own, number: assign_block(jax.random.fold_in(splits[3], 2), own, number, TR_DEV, DEVICES, 1, CAP, 2))(dest_keys, dest_turns).reshape((TRACES, 1))
    bins = set_ends(jax.random.randint(splits[4], (TRACES,), 0, REC_DEV * SHOT_DEV), jax.random.fold_in(splits[4], 1), 0, (REC_DEV * SHOT_DEV) - 1).astype(jnp.int32)
    return dict(data=data, traces=traces, weight=weight, dest=dest, bins=bins)


def make_table():
    steps_n = jnp.arange(NT, dtype=jnp.int32)
    columns = []
    for freq in (NT // 16, NT // 8):
        phase = ((freq * steps_n) % NT).astype(jnp.float32) * jnp.float32(2.0 * math.pi / NT)
        columns.append(jnp.cos(phase))
        columns.append(-jnp.sin(phase))
    return jnp.stack(columns, axis=1) * jnp.float32(NT ** -0.5)


def reference(data, traces, weight, dest, bins):
    spectra = jnp.dot(traces * weight[:, None], make_table(), precision=lax.Precision.HIGHEST)
    owner = dest[:, 0]
    row_idx = (owner // N_SHOT) * REC_DEV + bins // SHOT_DEV
    col_idx = (owner % N_SHOT) * SHOT_DEV + bins % SHOT_DEV
    flat_idx = (row_idx * NN + col_idx).astype(jnp.int32)
    full = data.astype(jnp.float32).reshape(4, NN * NN).at[:, flat_idx].add(spectra.T)
    binned = full.reshape(4, NN, NN).astype(jnp.bfloat16)
    total_re = jnp.zeros((2, NN, NN), jnp.float32)
    total_im = jnp.zeros((2, NN, NN), jnp.float32)
    for step in range(STEPS):
        panel = step * N_SHOT // STEPS
        cols = binned[:, :, panel * SHOT_DEV:(panel + 1) * SHOT_DEV].astype(jnp.float32).reshape(2, 2, NN, SHOT_DEV)
        rows = binned[:, panel * SHOT_DEV:(panel + 1) * SHOT_DEV, :].astype(jnp.float32).reshape(2, 2, SHOT_DEV, NN)
        total_re = total_re + jnp.einsum('frk,fkc->frc', cols[:, 0], rows[:, 0]) - jnp.einsum('frk,fkc->frc', cols[:, 1], rows[:, 1])
        total_im = total_im + jnp.einsum('frk,fkc->frc', cols[:, 0], rows[:, 1]) + jnp.einsum('frk,fkc->frc', cols[:, 1], rows[:, 0])
    factor = jnp.float32((2 * STEPS * SHOT_DEV) ** -0.5)
    multiples = jnp.stack([total_re, total_im], axis=1).reshape(4, NN, NN) * factor
    return binned, multiples
```

```python
import functools
import math

import jax
import jax.numpy as jnp
import numpy as np
from jax import lax
from jax.experimental import pallas as pl
from jax.experimental.pallas import tpu as pltpu
from jax.sharding import PartitionSpec as P

MESH = pl.DeviceIdType.MESH
SLOTS = 8
PERIOD = 128
CHUNKS = 16
STRETCH = 2

TREE = {
    (0, 0): ("b", "+y", "-y"),
    (3, 0): ("b",),
    (0, 1): ("f", "+y"),
    (1, 1): ("f", "-y"),
    (0, 3): ("b",),
    (3, 3): ("b",),
    (2, 3): ("-y",),
    (0, 2): ("f", "b"),
    (1, 2): ("+y",),
    (3, 2): ("-y",),
}
STEP = {"f": (1, 0), "b": (3, 0), "+y": (0, 1), "-y": (0, 3)}


def tree_depths():
    depths, front = {(0, 0): 0}, [(0, 0)]
    while front:
        at = front.pop(0)
        for way in TREE.get(at, ()):
            to = ((at[0] + STEP[way][0]) % 4, (at[1] + STEP[way][1]) % 4)
            assert to not in depths
            depths[to] = depths[at] + 1
            front.append(to)
    assert len(depths) == 16
    return depths


DEPTHS = tree_depths()


def table_t():
    n = np.arange(PERIOD)
    rows = []
    for freq in (128, 256):
        angle = (freq * n % 2048) * (2.0 * math.pi / 2048)
        rows += [np.cos(angle), -np.sin(angle)]
    rows = np.stack(rows) * 2048**-0.5
    return np.concatenate([rows, np.zeros((4, PERIOD))]).astype(np.float32)


def member(index, members):
    found = jnp.int32(0)
    for one in members:
        found = found + jnp.where(index == one, 1, 0)
    return found


def kernel(
    table, weight, dest, bins, data_hbm, traces_hbm, binned_hbm, mult_hbm,
    traces_v, data_v, send_a, recv_a, send_b, recv_b, rows_1h, cols_1h, cbuf, rbuf, binned_v, out_v,
    in_sem, a_send, a_recv, b_send, b_recv, c_send, c_recv, r_send, r_recv, out_sem,
):
    r = lax.axis_index("rcv")
    s = lax.axis_index("shot")
    x, y = s // 4, s % 4
    z, core = r // 2, r % 2
    f32, bf16 = jnp.float32, jnp.bfloat16

    trace_in = [
        pltpu.make_async_copy(traces_hbm.at[pl.ds(128 * i, 128)], traces_v.at[pl.ds(128 * i, 128)], in_sem.at[i])
        for i in range(4)
    ]
    data_in = pltpu.make_async_copy(data_hbm, data_v, in_sem.at[4])
    for one in trace_in:
        one.start()
    data_in.start()

    barrier = pltpu.get_barrier_semaphore()
    for k in range(1, 16):
        pl.semaphore_signal(barrier, inc=1, device_id=(r, lax.rem(s + k, 16)), device_id_type=MESH)
    for k in range(1, 8):
        pl.semaphore_signal(barrier, inc=1, device_id=(lax.rem(r + k, 8), s), device_id_type=MESH)

    owner = dest[...]
    owner = (owner & 15) * 8 + (owner >> 4)
    owner_1h = jnp.where(lax.broadcasted_iota(jnp.int32, (128, 512), 0) == owner, 1.0, 0.0)
    before = jnp.where(
        lax.broadcasted_iota(jnp.int32, (512, 512), 0) < lax.broadcasted_iota(jnp.int32, (512, 512), 1), 1.0, 0.0
    ).astype(bf16)
    owner_1h_b = owner_1h.astype(bf16)
    earlier = jnp.dot(owner_1h_b, before, preferred_element_type=f32)
    slot = jnp.sum(owner_1h * earlier, axis=0, keepdims=True)
    in_slot = lax.broadcasted_iota(jnp.int32, (SLOTS, 512), 0).astype(f32) == slot

    spectra = []
    for i in range(4):
        trace_in[i].wait()
        folded = traces_v[pl.ds(128 * i, 128), 0:PERIOD]
        for b in range(1, 16):
            folded = folded + traces_v[pl.ds(128 * i, 128), PERIOD * b : PERIOD * (b + 1)]
        spectra.append(
            lax.dot_general(
                table[...], folded, (((1,), (1,)), ((), ())),
                precision=lax.Precision.HIGHEST, preferred_element_type=f32,
            )
        )
    spectra = jnp.concatenate(spectra, axis=1)[0:4] * weight[...]
    high = spectra.astype(bf16).astype(f32)
    low = (spectra - high).astype(bf16).astype(f32)
    place = bins[...]
    words = [high[w : w + 1] for w in range(4)] + [low[w : w + 1] for w in range(4)]
    words += [(place >> 16).astype(f32), ((place >> 8) & 255).astype(f32), (place & 255).astype(f32)]
    listing = [jnp.where(in_slot, word, 0.0) for word in words]
    listing.append(jnp.zeros((128 - SLOTS * len(words), 512), f32))
    listing = jnp.concatenate(listing, axis=0).astype(bf16)
    send_a[...] = lax.dot_general(owner_1h_b, listing, (((1,), (1,)), ((), ())), preferred_element_type=f32)

    pl.semaphore_wait(barrier, 22)

    def copy_a(k):
        to = lax.rem(s + k, 16)
        return pltpu.make_async_remote_copy(
            src_ref=send_a.at[pl.ds(to * 8, 8)], dst_ref=recv_a.at[pl.ds(s * 8, 8)],
            send_sem=a_send.at[k - 1], recv_sem=a_recv.at[k - 1],
            device_id=(r, to), device_id_type=MESH,
        )

    def copy_b(k):
        to = lax.rem(r + k, 8)
        return pltpu.make_async_remote_copy(
            src_ref=send_b.at[pl.ds(to * 16, 16)], dst_ref=recv_b.at[pl.ds(r * 16, 16)],
            send_sem=b_send.at[k - 1], recv_sem=b_recv.at[k - 1],
            device_id=(to, s), device_id_type=MESH,
        )

    for k in range(1, 16):
        copy_a(k).start()
    own = pl.ds(pl.multiple_of(s * 8, 8), 8)
    recv_a[own] = send_a[own]
    for k in range(1, 16):
        copy_a(k).wait()
    for k in range(8):
        send_b[16 * k : 16 * (k + 1)] = recv_a[pl.ds(k, 16, stride=8)]
    for k in range(1, 8):
        copy_b(k).start()
    own = pl.ds(pl.multiple_of(r * 16, 16), 16)
    recv_b[own] = send_b[own]
    for k in range(1, 8):
        copy_b(k).wait()

    got = recv_b[...]
    got_t = jnp.transpose(got)
    for slot_at in range(SLOTS):
        k_at = pl.ds(128 * slot_at, 128)
        row = got_t[64 + slot_at : 65 + slot_at] * 256.0 + got_t[72 + slot_at : 73 + slot_at]
        rows_1h[:, k_at] = jnp.where(
            lax.broadcasted_iota(jnp.int32, (512, 128), 0).astype(f32) == row, 1.0, 0.0
        ).astype(bf16)
        column = got[:, 80 + slot_at : 81 + slot_at]
        at_column = lax.broadcasted_iota(jnp.int32, (128, 256), 1).astype(f32) == column
        for w in range(8):
            value = got[:, 8 * w + slot_at : 8 * w + slot_at + 1]
            cols_1h[w, k_at] = jnp.where(at_column, value, 0.0).astype(bf16)
    data_in.wait()
    for w in range(4):
        added = jnp.dot(rows_1h[...], cols_1h[w], preferred_element_type=f32)
        added = added + jnp.dot(rows_1h[...], cols_1h[w + 4], preferred_element_type=f32)
        binned_v[w] = (data_v[w].astype(f32) + added).astype(bf16)

    binned_out = pltpu.make_async_copy(binned_v, binned_hbm, out_sem.at[0])
    binned_out.start()

    @pl.when(y == 0)
    def _():
        cbuf[x] = binned_v[...]

    @pl.when(core == 0)
    def _():
        rbuf[z] = binned_v[:, 0:256, :]

    streams = []
    for p in range(4):
        for v in range(2):
            dx = lax.rem(x - p + 4, 4) if v == 0 else lax.rem(p - x + 4, 4)
            at = dx * 4 + y
            depth = jnp.int32(0)
            for node, value in DEPTHS.items():
                depth = depth + jnp.where(at == node[0] * 4 + node[1], value, 0)
            ways = {}
            for way in STEP:
                ways[way] = member(at, [n[0] * 4 + n[1] for n in TREE if way in TREE[n]])
            streams.append((p, v, depth, ways))
    up, down = lax.rem(x + 1, 4), lax.rem(x + 3, 4)

    def target(way, v):
        if way == "+y":
            return (r, x * 4 + lax.rem(y + 1, 4))
        if way == "-y":
            return (r, x * 4 + lax.rem(y + 3, 4))
        return (r, (up if (way == "f") == (v == 0) else down) * 4 + y)

    way_index = {way: i for i, way in enumerate(STEP)}

    def column_copy(p, v, j, way):
        comp = (j // 8) * 2 + lax.rem(j, 2)
        start = v * 256 + lax.rem(j // 2, 4) * 64
        ref = cbuf.at[p, comp, pl.ds(pl.multiple_of(start, 64), 64)]
        return pltpu.make_async_remote_copy(
            src_ref=ref, dst_ref=ref, send_sem=c_send.at[2 * p + v, way_index[way]],
            recv_sem=c_recv.at[2 * p + v, j], device_id=target(way, v), device_id_type=MESH,
        )

    z_up = (lax.rem(z + 1, 4) * 2 + core, s)
    z_down = (lax.rem(z + 3, 4) * 2 + core, s)
    z_core = (z * 2 + 1 - core, s)

    def row_copy(p, k, way):
        ref = rbuf.at[p, k]
        return pltpu.make_async_remote_copy(
            src_ref=ref, dst_ref=ref, send_sem=r_send.at[p, way], recv_sem=r_recv.at[p, k],
            device_id=(z_up, z_down, z_core)[way], device_id_type=MESH,
        )

    row_roles = []
    for p in range(4):
        dz = lax.rem(z - p + 4, 4)
        row_roles.append((p, dz, jnp.where(dz == 3, 1, dz) + core))

    @pl.loop(0, CHUNKS + 4 * STRETCH)
    def _(t):
        for p, v, depth, ways in streams:
            j = t - depth * STRETCH

            @pl.when((j >= 0) & (j < CHUNKS))
            def _():
                @pl.when(depth > 0)
                def _():
                    column_copy(p, v, j, "f").wait_recv()

                for way in STEP:
                    @pl.when(ways[way] == 1)
                    def _():
                        column_copy(p, v, j, way).start()

        for p, dz, depth in row_roles:
            k = t // 2 - depth

            @pl.when((lax.rem(t, 2) == 0) & (k >= 0) & (k < 4))
            def _():
                @pl.when(depth > 0)
                def _():
                    row_copy(p, k, 0).wait_recv()

                @pl.when(core == 0)
                def _():
                    row_copy(p, k, 2).start()

                    @pl.when((dz == 0) | ((dz == 1) & (k < 2)))
                    def _():
                        row_copy(p, k, 0).start()

                    @pl.when((dz == 0) | ((dz == 3) & (k >= 2)))
                    def _():
                        row_copy(p, k, 1).start()

    factor = 2048**-0.5
    for f in range(2):
        @pl.loop(0, 4)
        def _(i):
            at = pl.ds(pl.multiple_of(i * 128, 128), 128)
            re = jnp.zeros((128, 256), f32)
            im = jnp.zeros((128, 256), f32)
            for p in range(4):
                c_re, c_im = cbuf[p, 2 * f, at], cbuf[p, 2 * f + 1, at]
                r_re, r_im = rbuf[p, 2 * f], rbuf[p, 2 * f + 1]
                re = re + jnp.dot(c_re, r_re, preferred_element_type=f32)
                re = re - jnp.dot(c_im, r_im, preferred_element_type=f32)
                im = im + jnp.dot(c_re, r_im, preferred_element_type=f32)
                im = im + jnp.dot(c_im, r_re, preferred_element_type=f32)
            out_v[2 * f, at] = re * factor
            out_v[2 * f + 1, at] = im * factor

        pltpu.make_async_copy(out_v.at[pl.ds(2 * f, 2)], mult_hbm.at[pl.ds(2 * f, 2)], out_sem.at[1 + f]).start()

    for p, v, depth, ways in streams:
        for way in STEP:
            @pl.when(ways[way] == 1)
            def _():
                half = cbuf.at[p, :, pl.ds(v * 256, 256)]
                pltpu.make_async_remote_copy(
                    src_ref=half, dst_ref=half, send_sem=c_send.at[2 * p + v, way_index[way]],
                    recv_sem=c_recv.at[2 * p + v, 0], device_id=target(way, v), device_id_type=MESH,
                ).wait_send()

    def row_wait(p, ref, way):
        pltpu.make_async_remote_copy(
            src_ref=ref, dst_ref=ref, send_sem=r_send.at[p, way], recv_sem=r_recv.at[p, 0],
            device_id=(z_up, z_down, z_core)[way], device_id_type=MESH,
        ).wait_send()

    for p, dz, depth in row_roles:
        @pl.when(core == 0)
        def _():
            row_wait(p, rbuf.at[p], 2)

            @pl.when(dz == 0)
            def _():
                row_wait(p, rbuf.at[p], 0)
                row_wait(p, rbuf.at[p], 1)

            @pl.when(dz == 1)
            def _():
                row_wait(p, rbuf.at[p, pl.ds(0, 2)], 0)

            @pl.when(dz == 3)
            def _():
                row_wait(p, rbuf.at[p, pl.ds(2, 2)], 1)

    binned_out.wait()
    for f in range(2):
        pltpu.make_async_copy(out_v.at[pl.ds(2 * f, 2)], mult_hbm.at[pl.ds(2 * f, 2)], out_sem.at[1 + f]).wait()


def body(data, traces, weight, dest, bins):
    f32, bf16 = jnp.float32, jnp.bfloat16
    vmem = pl.BlockSpec(memory_space=pltpu.VMEM)
    hbm = pl.BlockSpec(memory_space=pl.ANY)
    dma = pltpu.SemaphoreType.DMA
    return pl.pallas_call(
        kernel,
        out_shape=(
            jax.ShapeDtypeStruct((4, 512, 256), bf16),
            jax.ShapeDtypeStruct((4, 512, 256), f32),
        ),
        in_specs=[vmem, vmem, vmem, vmem, hbm, hbm],
        out_specs=(hbm, hbm),
        scratch_shapes=[
            pltpu.VMEM((512, 2048), f32),
            pltpu.VMEM((4, 512, 256), bf16),
            pltpu.VMEM((128, 128), f32),
            pltpu.VMEM((128, 128), f32),
            pltpu.VMEM((128, 128), f32),
            pltpu.VMEM((128, 128), f32),
            pltpu.VMEM((512, 1024), bf16),
            pltpu.VMEM((8, 1024, 256), bf16),
            pltpu.VMEM((4, 4, 512, 256), bf16),
            pltpu.VMEM((4, 4, 256, 256), bf16),
            pltpu.VMEM((4, 512, 256), bf16),
            pltpu.VMEM((4, 512, 256), f32),
            dma((5,)),
            dma((15,)),
            dma((15,)),
            dma((7,)),
            dma((7,)),
            dma((8, 4)),
            dma((8, CHUNKS)),
            dma((4, 3)),
            dma((4, 4)),
            dma((3,)),
        ],
        compiler_params=pltpu.CompilerParams(
            collective_id=0, has_side_effects=True, vmem_limit_bytes=40 * 2**20
        ),
        cost_estimate=pl.CostEstimate(flops=5 * 10**9, bytes_accessed=9 * 2**20, transcendentals=0),
    )(
        jnp.asarray(table_t()),
        weight.reshape(1, 512),
        dest.reshape(1, 512),
        bins.reshape(1, 512),
        data,
        traces,
    )


def solution(mesh):
    placed = (
        P(None, "rcv", "shot"),
        P(("rcv", "shot"), None),
        P(("rcv", "shot")),
        P(("rcv", "shot"), None),
        P(("rcv", "shot")),
    )
    return jax.shard_map(
        body,
        mesh=mesh,
        in_specs=placed,
        out_specs=(P(None, "rcv", "shot"), P(None, "rcv", "shot")),
        check_vma=False,
    )
```

```python
import functools
import math

import jax
import jax.numpy as jnp
import numpy as np
from jax import lax
from jax.experimental import pallas as pl
from jax.experimental.pallas import tpu as pltpu
from jax.sharding import PartitionSpec as P

MESH = pl.DeviceIdType.MESH
SLOTS = 8
PERIOD = 128
CHUNKS = 16
STRETCH = 3

TREE = {
    (0, 0): ("b", "+y", "-y"),
    (3, 0): ("b",),
    (0, 1): ("f", "+y"),
    (1, 1): ("f", "-y"),
    (0, 3): ("b",),
    (3, 3): ("b",),
    (2, 3): ("-y",),
    (0, 2): ("f", "b"),
    (1, 2): ("+y",),
    (3, 2): ("-y",),
}
STEP = {"f": (1, 0), "b": (3, 0), "+y": (0, 1), "-y": (0, 3)}


def tree_depths():
    depths, front = {(0, 0): 0}, [(0, 0)]
    while front:
        at = front.pop(0)
        for way in TREE.get(at, ()):
            to = ((at[0] + STEP[way][0]) % 4, (at[1] + STEP[way][1]) % 4)
            assert to not in depths
            depths[to] = depths[at] + 1
            front.append(to)
    assert len(depths) == 16
    return depths


DEPTHS = tree_depths()


def table_t():
    n = np.arange(PERIOD)
    rows = []
    for freq in (128, 256):
        angle = (freq * n % 2048) * (2.0 * math.pi / 2048)
        rows += [np.cos(angle), -np.sin(angle)]
    rows = np.stack(rows) * 2048**-0.5
    return np.concatenate([rows, np.zeros((4, PERIOD))]).astype(np.float32)


def member(index, members):
    found = jnp.int32(0)
    for one in members:
        found = found + jnp.where(index == one, 1, 0)
    return found


def kernel(
    table_hbm, weight_hbm, dest_hbm, bins_hbm, data_hbm, traces_hbm, binned_hbm, mult_hbm,
    table, weight, dest, bins, traces_v, data_v, send_a, recv_a, send_b, recv_b, rows_1h, cols_1h,
    cbuf, rbuf, rbuf_0, corr_c, corr_r, corr_own, delta, binned_v, out_v,
    in_sem, a_send, a_recv, b_send, b_recv, c_send, c_recv, r_send, r_recv,
    cc_send, cc_recv, cr_send, cr_recv, out_sem,
):
    r = lax.axis_index("rcv")
    s = lax.axis_index("shot")
    x, y = s // 4, s % 4
    z, core = r // 2, r % 2
    f32, bf16 = jnp.float32, jnp.bfloat16

    small_in = [
        pltpu.make_async_copy(one, to, in_sem.at[5 + i])
        for i, (one, to) in enumerate(((dest_hbm, dest), (table_hbm, table), (weight_hbm, weight), (bins_hbm, bins)))
    ]
    trace_in = [
        pltpu.make_async_copy(traces_hbm.at[pl.ds(128 * i, 128)], traces_v.at[pl.ds(128 * i, 128)], in_sem.at[i])
        for i in range(4)
    ]
    data_in = pltpu.make_async_copy(data_hbm, data_v, in_sem.at[4])
    for one in small_in:
        one.start()
    for one in trace_in:
        one.start()
    data_in.start()

    barrier = pltpu.get_barrier_semaphore()
    for k in range(1, 16):
        pl.semaphore_signal(barrier, inc=1, device_id=(r, lax.rem(s + k, 16)), device_id_type=MESH)
    for k in range(1, 8):
        pl.semaphore_signal(barrier, inc=1, device_id=(lax.rem(r + k, 8), s), device_id_type=MESH)

    for one in small_in:
        one.wait()
    owner = dest[...]
    owner = (owner & 15) * 8 + (owner >> 4)
    owner_1h = jnp.where(lax.broadcasted_iota(jnp.int32, (128, 512), 0) == owner, 1.0, 0.0)
    before = jnp.where(
        lax.broadcasted_iota(jnp.int32, (512, 512), 0) < lax.broadcasted_iota(jnp.int32, (512, 512), 1), 1.0, 0.0
    ).astype(bf16)
    owner_1h_b = owner_1h.astype(bf16)
    earlier = jnp.dot(owner_1h_b, before, preferred_element_type=f32)
    slot = jnp.sum(owner_1h * earlier, axis=0, keepdims=True)
    in_slot = lax.broadcasted_iota(jnp.int32, (SLOTS, 512), 0).astype(f32) == slot

    spectra = []
    for i in range(4):
        trace_in[i].wait()
        folded = traces_v[pl.ds(128 * i, 128), 0:PERIOD]
        for b in range(1, 16):
            folded = folded + traces_v[pl.ds(128 * i, 128), PERIOD * b : PERIOD * (b + 1)]
        spectra.append(
            lax.dot_general(
                table[...], folded, (((1,), (1,)), ((), ())),
                precision=lax.Precision.HIGHEST, preferred_element_type=f32,
            )
        )
    spectra = jnp.concatenate(spectra, axis=1)[0:4] * weight[...]
    high = spectra.astype(bf16).astype(f32)
    low = (spectra - high).astype(bf16).astype(f32)
    place = bins[...]
    words = [high[w : w + 1] for w in range(4)] + [low[w : w + 1] for w in range(4)]
    words += [(place >> 16).astype(f32), ((place >> 8) & 255).astype(f32), (place & 255).astype(f32)]
    listing = [jnp.where(in_slot, word, 0.0) for word in words]
    listing.append(jnp.zeros((128 - SLOTS * len(words), 512), f32))
    listing = jnp.concatenate(listing, axis=0).astype(bf16)
    send_a[...] = lax.dot_general(owner_1h_b, listing, (((1,), (1,)), ((), ())), preferred_element_type=f32)

    data_in.wait()

    @pl.when(y == 0)
    def _():
        cbuf[x, 0:2] = data_v[0:2]

    @pl.when(core == 0)
    def _():
        rbuf[z, 0:2] = data_v[0:2, 0:256]

    streams = []
    for p in range(4):
        for v in range(2):
            dx = lax.rem(x - p + 4, 4) if v == 0 else lax.rem(p - x + 4, 4)
            at = dx * 4 + y
            depth = jnp.int32(0)
            for node, value in DEPTHS.items():
                depth = depth + jnp.where(at == node[0] * 4 + node[1], value, 0)
            ways = {}
            for way in STEP:
                ways[way] = member(at, [n[0] * 4 + n[1] for n in TREE if way in TREE[n]])
            streams.append((p, v, depth, ways))
    up, down = lax.rem(x + 1, 4), lax.rem(x + 3, 4)

    def target(way, v):
        if way == "+y":
            return (r, x * 4 + lax.rem(y + 1, 4))
        if way == "-y":
            return (r, x * 4 + lax.rem(y + 3, 4))
        return (r, (up if (way == "f") == (v == 0) else down) * 4 + y)

    way_index = {way: i for i, way in enumerate(STEP)}

    def column_copy(p, v, j, way):
        comp = (j // 8) * 2 + lax.rem(j, 2)
        start = v * 256 + lax.rem(j // 2, 4) * 64
        ref = cbuf.at[p, comp, pl.ds(pl.multiple_of(start, 64), 64)]
        return pltpu.make_async_remote_copy(
            src_ref=ref, dst_ref=ref, send_sem=c_send.at[2 * p + v, way_index[way]],
            recv_sem=c_recv.at[2 * p + v, j], device_id=target(way, v), device_id_type=MESH,
        )

    z_up = (lax.rem(z + 1, 4) * 2 + core, s)
    z_down = (lax.rem(z + 3, 4) * 2 + core, s)
    z_core = (z * 2 + 1 - core, s)

    def row_copy(p, k, way):
        ref = rbuf.at[p, k // 2, pl.ds(pl.multiple_of(lax.rem(k, 2) * 128, 128), 128)]
        return pltpu.make_async_remote_copy(
            src_ref=ref, dst_ref=ref, send_sem=r_send.at[p, way], recv_sem=r_recv.at[p, k],
            device_id=(z_up, z_down, z_core)[way], device_id_type=MESH,
        )

    row_roles = []
    for p in range(4):
        dz = lax.rem(z - p + 4, 4)
        row_roles.append((p, dz, jnp.where(dz == 3, 1, dz) + core))

    def step(t):
        for p, v, depth, ways in streams:
            j = t - depth * STRETCH

            @pl.when((j >= 0) & (j < CHUNKS))
            def _():
                @pl.when(depth > 0)
                def _():
                    column_copy(p, v, j, "f").wait_recv()

                for way in STEP:
                    @pl.when(ways[way] == 1)
                    def _():
                        column_copy(p, v, j, way).start()

        for p, dz, depth in row_roles:
            at = t - depth * STRETCH
            k = jnp.where(at >= 8, at - 4, at)

            @pl.when((at >= 0) & (k < 8) & ((at < 4) | (at >= 8)))
            def _():
                @pl.when(depth > 0)
                def _():
                    row_copy(p, k, 0).wait_recv()

                @pl.when(core == 0)
                def _():
                    row_copy(p, k, 2).start()

                    @pl.when((dz == 0) | ((dz == 1) & (lax.rem(k, 2) == 0)))
                    def _():
                        row_copy(p, k, 0).start()

                    @pl.when((dz == 0) | ((dz == 3) & (lax.rem(k, 2) == 1)))
                    def _():
                        row_copy(p, k, 1).start()

    def steps(first, last):
        @pl.loop(first, last)
        def _(t):
            step(t)

    def copy_a(k):
        to = lax.rem(s + k, 16)
        return pltpu.make_async_remote_copy(
            src_ref=send_a.at[pl.ds(to * 8, 8)], dst_ref=recv_a.at[pl.ds(s * 8, 8)],
            send_sem=a_send.at[k - 1], recv_sem=a_recv.at[k - 1],
            device_id=(r, to), device_id_type=MESH,
        )

    def copy_b(k):
        to = lax.rem(r + k, 8)
        return pltpu.make_async_remote_copy(
            src_ref=send_b.at[pl.ds(to * 16, 16)], dst_ref=recv_b.at[pl.ds(r * 16, 16)],
            send_sem=b_send.at[k - 1], recv_sem=b_recv.at[k - 1],
            device_id=(to, s), device_id_type=MESH,
        )

    def corr_column(k):
        return pltpu.make_async_remote_copy(
            src_ref=corr_own, dst_ref=corr_c.at[x], send_sem=cc_send.at[k - 1], recv_sem=cc_recv.at[x],
            device_id=(r, lax.rem(s + k, 16)), device_id_type=MESH,
        )

    def corr_row(k):
        return pltpu.make_async_remote_copy(
            src_ref=corr_own, dst_ref=corr_r.at[z], send_sem=cr_send.at[k - 1], recv_sem=cr_recv.at[z],
            device_id=(lax.rem(r + k, 8), s), device_id_type=MESH,
        )

    def build_rows(got_t, count):
        for slot_at in range(SLOTS):
            high_row = got_t[64 + slot_at : 65 + slot_at]
            low_row = got_t[72 + slot_at : 73 + slot_at]
            for h in range(count // 256):
                row = jnp.where(high_row == float(h), low_row, -1.0).astype(bf16)
                rows_1h[256 * h : 256 * (h + 1), 128 * slot_at : 128 * (slot_at + 1)] = jnp.where(
                    iota_row == row, jnp.bfloat16(1), jnp.bfloat16(0)
                )

    def build_cols(got, f):
        for slot_at in range(SLOTS):
            column = got[:, 80 + slot_at : 81 + slot_at]
            at_column = iota_col == column
            for i, w in enumerate((2 * f, 2 * f + 1, 4 + 2 * f, 5 + 2 * f)):
                value = got[:, 8 * w + slot_at : 8 * w + slot_at + 1]
                cols_1h[i, 128 * slot_at : 128 * (slot_at + 1)] = jnp.where(at_column, value, jnp.bfloat16(0))

    def added(i, count):
        total = jnp.dot(rows_1h[0:count], cols_1h[i], preferred_element_type=f32)
        return total + jnp.dot(rows_1h[0:count], cols_1h[i + 2], preferred_element_type=f32)

    iota_row = lax.broadcasted_iota(jnp.int32, (256, 128), 0).astype(f32).astype(bf16)
    iota_col = lax.broadcasted_iota(jnp.int32, (128, 256), 1).astype(f32).astype(bf16)

    pl.semaphore_wait(barrier, 22)

    for k in range(1, 16):
        copy_a(k).start()
    own = pl.ds(pl.multiple_of(s * 8, 8), 8)
    recv_a[own] = send_a[own]
    steps(0, 4)
    for k in range(1, 16):
        copy_a(k).wait()
    for k in range(8):
        send_b[16 * k : 16 * (k + 1)] = recv_a[pl.ds(k, 16, stride=8)]
    for k in range(1, 8):
        copy_b(k).start()
    own = pl.ds(pl.multiple_of(r * 16, 16), 16)
    recv_b[own] = send_b[own]
    steps(4, 7)
    for k in range(1, 8):
        copy_b(k).wait()
    corr_own[...] = recv_b[...].astype(bf16)

    @pl.when(y == 0)
    def _():
        for k in range(1, 16):
            corr_column(k).start()
        corr_c[x] = corr_own[...]

    @pl.when(core == 0)
    def _():
        for k in range(1, 8):
            corr_row(k).start()
        corr_r[z] = corr_own[...]

    steps(7, 8)

    build_rows(jnp.transpose(recv_b[...]), 512)
    for f in (1, 0):
        build_cols(corr_own[...], f)
        for i in range(2):
            binned_v[2 * f + i] = (data_v[2 * f + i].astype(f32) + added(i, 512)).astype(bf16)
        if f == 1:
            @pl.when(y == 0)
            def _():
                cbuf[x, 2:4] = binned_v[2:4]

            @pl.when(core == 0)
            def _():
                rbuf[z, 2:4] = binned_v[2:4, 0:256]

            steps(8, 9)
    binned_out = pltpu.make_async_copy(binned_v, binned_hbm, out_sem.at[0])
    binned_out.start()
    steps(9, 12)

    for p in range(4):
        @pl.when((y != 0) | (x != p))
        def _():
            pltpu.make_async_remote_copy(
                src_ref=corr_own, dst_ref=corr_c.at[p], send_sem=cc_send.at[0], recv_sem=cc_recv.at[p],
                device_id=(r, lax.rem(s + 1, 16)), device_id_type=MESH,
            ).wait_recv()

        @pl.when((core != 0) | (z != p))
        def _():
            pltpu.make_async_remote_copy(
                src_ref=corr_own, dst_ref=corr_r.at[p], send_sem=cr_send.at[0], recv_sem=cr_recv.at[p],
                device_id=(lax.rem(r + 1, 8), s), device_id_type=MESH,
            ).wait_recv()

    @pl.loop(12, 16)
    def _(t):
        step(t)
        p = t - 12
        got = corr_r[p]
        build_rows(jnp.transpose(got.astype(f32)), 256)
        build_cols(got, 0)
        for i in range(2):
            rbuf_0[p, i] = (rbuf[p, i].astype(f32) + added(i, 256)).astype(bf16)

    @pl.loop(16, 20)
    def _(t):
        step(t)
        p = t - 16
        got = corr_c[p]
        build_rows(jnp.transpose(got.astype(f32)), 512)
        build_cols(got, 0)
        for i in range(2):
            delta[p, i] = added(i, 512)

    factor = 2048**-0.5

    def product(f, c_re, c_im):
        rows = c_re[0].shape[0]
        re = jnp.zeros((rows, 256), f32)
        im = jnp.zeros((rows, 256), f32)
        for p in range(4):
            r_re, r_im = (rbuf_0[p, 0], rbuf_0[p, 1]) if f == 0 else (rbuf[p, 2], rbuf[p, 3])
            re = re + jnp.dot(c_re[p], r_re, preferred_element_type=f32)
            re = re - jnp.dot(c_im[p], r_im, preferred_element_type=f32)
            im = im + jnp.dot(c_re[p], r_im, preferred_element_type=f32)
            im = im + jnp.dot(c_im[p], r_re, preferred_element_type=f32)
        return re * factor, im * factor

    @pl.loop(20, 24)
    def _(t):
        step(t)
        at = pl.ds(pl.multiple_of((t - 20) * 128, 128), 128)
        c_re, c_im = [
            [(cbuf[p, i, at].astype(f32) + delta[p, i, at]).astype(bf16) for p in range(4)] for i in range(2)
        ]
        out_v[0, at], out_v[1, at] = product(0, c_re, c_im)

    mult_out = [
        pltpu.make_async_copy(out_v.at[pl.ds(2 * f, 2)], mult_hbm.at[pl.ds(2 * f, 2)], out_sem.at[1 + f])
        for f in range(2)
    ]
    mult_out[0].start()

    @pl.loop(24, 28)
    def _(t):
        step(t)
        ats = [pl.ds(pl.multiple_of(256 * v + (t - 24) * 64, 64), 64) for v in range(2)]
        c_re, c_im = [
            [jnp.concatenate([cbuf[p, i, at] for at in ats], axis=0) for p in range(4)] for i in (2, 3)
        ]
        re, im = product(1, c_re, c_im)
        for v in range(2):
            out_v[2, ats[v]] = re[64 * v : 64 * (v + 1)]
            out_v[3, ats[v]] = im[64 * v : 64 * (v + 1)]

    mult_out[1].start()

    for p, v, depth, ways in streams:
        for way in STEP:
            @pl.when(ways[way] == 1)
            def _():
                half = cbuf.at[p, :, pl.ds(v * 256, 256)]
                pltpu.make_async_remote_copy(
                    src_ref=half, dst_ref=half, send_sem=c_send.at[2 * p + v, way_index[way]],
                    recv_sem=c_recv.at[2 * p + v, 0], device_id=target(way, v), device_id_type=MESH,
                ).wait_send()

    def row_wait(p, ref, way):
        pltpu.make_async_remote_copy(
            src_ref=ref, dst_ref=ref, send_sem=r_send.at[p, way], recv_sem=r_recv.at[p, 0],
            device_id=(z_up, z_down, z_core)[way], device_id_type=MESH,
        ).wait_send()

    for p, dz, depth in row_roles:
        @pl.when(core == 0)
        def _():
            row_wait(p, rbuf.at[p], 2)

            @pl.when(dz == 0)
            def _():
                row_wait(p, rbuf.at[p], 0)
                row_wait(p, rbuf.at[p], 1)

            @pl.when(dz == 1)
            def _():
                row_wait(p, rbuf.at[p, pl.ds(0, 2)], 0)

            @pl.when(dz == 3)
            def _():
                row_wait(p, rbuf.at[p, pl.ds(2, 2)], 1)

    @pl.when(y == 0)
    def _():
        for k in range(1, 16):
            corr_column(k).wait_send()

    @pl.when(core == 0)
    def _():
        for k in range(1, 8):
            corr_row(k).wait_send()

    binned_out.wait()
    for one in mult_out:
        one.wait()


def body(data, traces, weight, dest, bins):
    f32, bf16 = jnp.float32, jnp.bfloat16
    hbm = pl.BlockSpec(memory_space=pl.ANY)
    dma = pltpu.SemaphoreType.DMA
    return pl.pallas_call(
        kernel,
        out_shape=(
            jax.ShapeDtypeStruct((4, 512, 256), bf16),
            jax.ShapeDtypeStruct((4, 512, 256), f32),
        ),
        in_specs=[pl.BlockSpec(memory_space=pltpu.HBM)] * 6,
        out_specs=(hbm, hbm),
        scratch_shapes=[
            pltpu.VMEM((8, 128), f32),
            pltpu.VMEM((1, 512), f32),
            pltpu.VMEM((1, 512), jnp.int32),
            pltpu.VMEM((1, 512), jnp.int32),
            pltpu.VMEM((512, 2048), f32),
            pltpu.VMEM((4, 512, 256), bf16),
            pltpu.VMEM((128, 128), f32),
            pltpu.VMEM((128, 128), f32),
            pltpu.VMEM((128, 128), f32),
            pltpu.VMEM((128, 128), f32),
            pltpu.VMEM((512, 1024), bf16),
            pltpu.VMEM((4, 1024, 256), bf16),
            pltpu.VMEM((4, 4, 512, 256), bf16),
            pltpu.VMEM((4, 4, 256, 256), bf16),
            pltpu.VMEM((4, 2, 256, 256), bf16),
            pltpu.VMEM((4, 128, 128), bf16),
            pltpu.VMEM((4, 128, 128), bf16),
            pltpu.VMEM((128, 128), bf16),
            pltpu.VMEM((4, 2, 512, 256), f32),
            pltpu.VMEM((4, 512, 256), bf16),
            pltpu.VMEM((4, 512, 256), f32),
            dma((9,)),
            dma((15,)),
            dma((15,)),
            dma((7,)),
            dma((7,)),
            dma((8, 4)),
            dma((8, CHUNKS)),
            dma((4, 3)),
            dma((4, 8)),
            dma((15,)),
            dma((4,)),
            dma((7,)),
            dma((4,)),
            dma((3,)),
        ],
        compiler_params=pltpu.CompilerParams(
            collective_id=0, has_side_effects=True, vmem_limit_bytes=60 * 2**20
        ),
        cost_estimate=pl.CostEstimate(flops=5 * 10**9, bytes_accessed=9 * 2**20, transcendentals=0),
    )(
        jnp.asarray(table_t()),
        weight.reshape(1, 512),
        dest.reshape(1, 512),
        bins.reshape(1, 512),
        data,
        traces,
    )


def solution(mesh):
    placed = (
        P(None, "rcv", "shot"),
        P(("rcv", "shot"), None),
        P(("rcv", "shot")),
        P(("rcv", "shot"), None),
        P(("rcv", "shot")),
    )
    return jax.shard_map(
        body,
        mesh=mesh,
        in_specs=placed,
        out_specs=(P(None, "rcv", "shot"), P(None, "rcv", "shot")),
        check_vma=False,
    )
```

```python
import functools
import math

import jax
import jax.numpy as jnp
import numpy as np
from jax import lax
from jax.experimental import pallas as pl
from jax.experimental.pallas import tpu as pltpu
from jax.sharding import PartitionSpec as P

MESH = pl.DeviceIdType.MESH
SLOTS = 8
PERIOD = 128
CHUNKS = 16
ROWS_LATE = 9
STRETCH = 3

TREE = {
    (0, 0): ("b", "+y", "-y"),
    (3, 0): ("b",),
    (0, 1): ("f", "+y"),
    (1, 1): ("f", "-y"),
    (0, 3): ("b",),
    (3, 3): ("b",),
    (2, 3): ("-y",),
    (0, 2): ("f", "b"),
    (1, 2): ("+y",),
    (3, 2): ("-y",),
}
STEP = {"f": (1, 0), "b": (3, 0), "+y": (0, 1), "-y": (0, 3)}


def tree_depths():
    depths, front = {(0, 0): 0}, [(0, 0)]
    while front:
        at = front.pop(0)
        for way in TREE.get(at, ()):
            to = ((at[0] + STEP[way][0]) % 4, (at[1] + STEP[way][1]) % 4)
            assert to not in depths
            depths[to] = depths[at] + 1
            front.append(to)
    assert len(depths) == 16
    return depths


DEPTHS = tree_depths()


def table_t():
    n = np.arange(PERIOD)
    rows = []
    for freq in (128, 256):
        angle = (freq * n % 2048) * (2.0 * math.pi / 2048)
        rows += [np.cos(angle), -np.sin(angle)]
    rows = np.stack(rows) * 2048**-0.5
    return np.concatenate([rows, np.zeros((4, PERIOD))]).astype(np.float32)


def kernel(
    table_hbm, weight_hbm, dest_hbm, bins_hbm, data_hbm, traces_hbm, binned_v, out_v,
    table, weight, dest, bins, traces_v, data_v, send_a, recv_a, send_b, recv_b, rows_1h, cols_1h,
    cbuf, rbuf, rbuf_0, corr_c, corr_r, corr_own, delta,
    in_sem, a_send, a_recv, b_send, b_recv, c_send, c_recv, r_send, r_recv,
    cc_send, cc_recv, cr_send, cr_recv,
):
    r = lax.axis_index("rcv")
    s = lax.axis_index("shot")
    x, y = s // 4, s % 4
    z, core = r // 2, r % 2
    f32, bf16 = jnp.float32, jnp.bfloat16

    small_in = [
        pltpu.make_async_copy(one, to, in_sem.at[5 + i])
        for i, (one, to) in enumerate(((dest_hbm, dest), (table_hbm, table), (weight_hbm, weight), (bins_hbm, bins)))
    ]
    trace_in = [
        pltpu.make_async_copy(traces_hbm.at[pl.ds(128 * i, 128)], traces_v.at[pl.ds(128 * i, 128)], in_sem.at[i])
        for i in range(4)
    ]
    data_in = pltpu.make_async_copy(data_hbm, data_v, in_sem.at[4])
    for one in small_in:
        one.start()
    for one in trace_in:
        one.start()
    data_in.start()

    barrier = pltpu.get_barrier_semaphore()
    for k in range(1, 16):
        pl.semaphore_signal(barrier, inc=1, device_id=(r, lax.rem(s + k, 16)), device_id_type=MESH)
    for k in range(1, 8):
        pl.semaphore_signal(barrier, inc=1, device_id=(lax.rem(r + k, 8), s), device_id_type=MESH)

    for one in small_in:
        one.wait()
    owner = dest[...]
    owner = (owner & 15) * 8 + (owner >> 4)
    owner_1h = jnp.where(lax.broadcasted_iota(jnp.int32, (128, 512), 0) == owner, 1.0, 0.0)
    before = jnp.where(
        lax.broadcasted_iota(jnp.int32, (512, 512), 0) < lax.broadcasted_iota(jnp.int32, (512, 512), 1), 1.0, 0.0
    ).astype(bf16)
    owner_1h_b = owner_1h.astype(bf16)
    earlier = jnp.dot(owner_1h_b, before, preferred_element_type=f32)
    slot = jnp.sum(owner_1h * earlier, axis=0, keepdims=True)
    in_slot = lax.broadcasted_iota(jnp.int32, (SLOTS, 512), 0).astype(f32) == slot

    spectra = []
    for i in range(4):
        trace_in[i].wait()
        folded = traces_v[pl.ds(128 * i, 128), 0:PERIOD]
        for b in range(1, 16):
            folded = folded + traces_v[pl.ds(128 * i, 128), PERIOD * b : PERIOD * (b + 1)]
        spectra.append(
            lax.dot_general(
                table[...], folded, (((1,), (1,)), ((), ())),
                precision=lax.Precision.HIGHEST, preferred_element_type=f32,
            )
        )
    spectra = jnp.concatenate(spectra, axis=1)[0:4] * weight[...]
    high = spectra.astype(bf16).astype(f32)
    low = (spectra - high).astype(bf16).astype(f32)
    place = bins[...]
    words = [high[0:1], high[1:2], low[0:1], low[1:2]]
    words += [(place >> 16).astype(f32), ((place >> 8) & 255).astype(f32), (place & 255).astype(f32)]
    words += [jnp.zeros_like(weight[...]), high[2:3], high[3:4], low[2:3], low[3:4]]
    listing = [jnp.where(in_slot, word, 0.0) for word in words]
    listing.append(jnp.zeros((128 - SLOTS * len(words), 512), f32))
    listing = jnp.concatenate(listing, axis=0).astype(bf16)
    send_a[...] = lax.dot_general(owner_1h_b, listing, (((1,), (1,)), ((), ())), preferred_element_type=f32)

    data_in.wait()

    @pl.when(y == 0)
    def _():
        cbuf[x, 0:2] = data_v[0:2]

    @pl.when(core == 0)
    def _():
        rbuf[z, 0:2] = data_v[0:2, 0:256]

    streams = [(dx, v, lax.rem(x + (4 - dx if v == 0 else dx), 4)) for dx in range(4) for v in range(2)]
    up, down = lax.rem(x + 1, 4), lax.rem(x + 3, 4)

    def target(way, v):
        if way == "+y":
            return (r, x * 4 + lax.rem(y + 1, 4))
        if way == "-y":
            return (r, x * 4 + lax.rem(y + 3, 4))
        return (r, (up if (way == "f") == (v == 0) else down) * 4 + y)

    way_index = {way: i for i, way in enumerate(STEP)}

    def column_copy(dx, v, p, j, way):
        comp = (j // 8) * 2 + lax.rem(j, 2)
        start = v * 256 + lax.rem(j // 2, 4) * 64
        ref = cbuf.at[p, comp, pl.ds(pl.multiple_of(start, 64), 64)]
        return pltpu.make_async_remote_copy(
            src_ref=ref, dst_ref=ref, send_sem=c_send.at[2 * dx + v, way_index[way]],
            recv_sem=c_recv.at[2 * p + v, j], device_id=target(way, v), device_id_type=MESH,
        )

    z_up = (lax.rem(z + 1, 4) * 2 + core, s)
    z_down = (lax.rem(z + 3, 4) * 2 + core, s)
    z_core = (z * 2 + 1 - core, s)

    def row_copy(p, k, way):
        ref = rbuf.at[p, k // 2, pl.ds(pl.multiple_of(lax.rem(k, 2) * 128, 128), 128)]
        return pltpu.make_async_remote_copy(
            src_ref=ref, dst_ref=ref, send_sem=r_send.at[p, way], recv_sem=r_recv.at[p, k],
            device_id=(z_up, z_down, z_core)[way], device_id_type=MESH,
        )

    row_panels = [lax.rem(z + 4 - dz, 4) for dz in range(4)]

    def within(t, low, high, first, last, act):
        if low <= first and last <= high:
            act()
        elif first < high and low < last:
            pl.when((t >= low) & (t < high))(act)

    def step(t, first, last):
        for row in range(4):
            @pl.when(y == row)
            def _():
                for dx, v, p in streams:
                    delay = DEPTHS[dx, row] * STRETCH

                    def pass_on():
                        if delay:
                            column_copy(dx, v, p, t - delay, "f").wait_recv()
                        for way in TREE.get((dx, row), ()):
                            column_copy(dx, v, p, t - delay, way).start()

                    within(t, delay, delay + CHUNKS, first, last, pass_on)

        for side in range(2):
            @pl.when(core == side)
            def _():
                for dz, p in enumerate(row_panels):
                    delay = (min(dz, 4 - dz) + side) * STRETCH
                    for begin, k_first in ((0, 0), (ROWS_LATE, 4)):
                        def pass_on():
                            k = t - delay - begin + k_first
                            if delay:
                                row_copy(p, k, 0).wait_recv()
                            if side == 0:
                                row_copy(p, k, 2).start()
                                if dz == 0:
                                    row_copy(p, k, 0).start()
                                    row_copy(p, k, 1).start()
                                elif dz == 1:
                                    pl.when(lax.rem(k, 2) == 0)(lambda: row_copy(p, k, 0).start())
                                elif dz == 3:
                                    pl.when(lax.rem(k, 2) == 1)(lambda: row_copy(p, k, 1).start())

                        within(t, delay + begin, delay + begin + 4, first, last, pass_on)

    def steps(first, last, work=None):
        if last == first + 1:
            step(first, first, last)
            return

        @pl.loop(first, last)
        def _(t):
            step(t, first, last)
            if work:
                work(t)

    def copy_a(k):
        to = lax.rem(s + k, 16)
        return pltpu.make_async_remote_copy(
            src_ref=send_a.at[pl.ds(to * 8, 8)], dst_ref=recv_a.at[pl.ds(s * 8, 8)],
            send_sem=a_send.at[k - 1], recv_sem=a_recv.at[k - 1],
            device_id=(r, to), device_id_type=MESH,
        )

    def copy_b(k):
        to = lax.rem(r + k, 8)
        return pltpu.make_async_remote_copy(
            src_ref=send_b.at[pl.ds(to * 16, 16)], dst_ref=recv_b.at[pl.ds(r * 16, 16)],
            send_sem=b_send.at[k - 1], recv_sem=b_recv.at[k - 1],
            device_id=(to, s), device_id_type=MESH,
        )

    def corr_column(k, along_x):
        to = lax.rem(x + k, 4) * 4 + y if along_x else x * 4 + lax.rem(y + k, 4)
        return pltpu.make_async_remote_copy(
            src_ref=corr_c.at[x], dst_ref=corr_c.at[x], send_sem=cc_send.at[k - 1 + 3 * along_x],
            recv_sem=cc_recv.at[x], device_id=(r, to), device_id_type=MESH,
        )

    def corr_arrived(p):
        pltpu.make_async_remote_copy(
            src_ref=corr_own, dst_ref=corr_c.at[p], send_sem=cc_send.at[0], recv_sem=cc_recv.at[p],
            device_id=(r, lax.rem(s + 1, 16)), device_id_type=MESH,
        ).wait_recv()

    def unpack(packed):
        return jnp.concatenate([packed[:, 0:64], packed[:, 64:128]], axis=0)

    def corr_row(k):
        return pltpu.make_async_remote_copy(
            src_ref=corr_own, dst_ref=corr_r.at[z], send_sem=cr_send.at[k - 1], recv_sem=cr_recv.at[z],
            device_id=(lax.rem(r + k, 8), s), device_id_type=MESH,
        )

    def build_rows(got_t, count):
        for slot_at in range(SLOTS):
            high_row = got_t[32 + slot_at : 33 + slot_at]
            low_row = got_t[40 + slot_at : 41 + slot_at]
            for h in range(count // 256):
                row = jnp.where(high_row == float(h), low_row, -1.0).astype(bf16)
                rows_1h[256 * h : 256 * (h + 1), 128 * slot_at : 128 * (slot_at + 1)] = jnp.where(
                    iota_row == row, jnp.bfloat16(1), jnp.bfloat16(0)
                )

    def build_cols(got, f):
        for slot_at in range(SLOTS):
            column = got[:, 48 + slot_at : 49 + slot_at]
            at_column = iota_col == column
            for i, w in enumerate(range(8 * f, 8 * f + 4)):
                value = got[:, 8 * w + slot_at : 8 * w + slot_at + 1]
                cols_1h[i, 128 * slot_at : 128 * (slot_at + 1)] = jnp.where(at_column, value, jnp.bfloat16(0))

    def added(i, at):
        total = jnp.dot(rows_1h[at], cols_1h[i], preferred_element_type=f32)
        return total + jnp.dot(rows_1h[at], cols_1h[i + 2], preferred_element_type=f32)

    iota_row = lax.broadcasted_iota(jnp.int32, (256, 128), 0).astype(f32).astype(bf16)
    iota_col = lax.broadcasted_iota(jnp.int32, (128, 256), 1).astype(f32).astype(bf16)

    pl.semaphore_wait(barrier, 22)

    for k in range(1, 16):
        copy_a(k).start()
    own = pl.ds(pl.multiple_of(s * 8, 8), 8)
    recv_a[own] = send_a[own]
    steps(0, 4)
    for k in range(1, 16):
        copy_a(k).wait()
    for k in range(8):
        send_b[16 * k : 16 * (k + 1)] = recv_a[pl.ds(k, 16, stride=8)]
    for k in range(1, 8):
        copy_b(k).start()
    own = pl.ds(pl.multiple_of(r * 16, 16), 16)
    recv_b[own] = send_b[own]
    steps(4, 7)
    for k in range(1, 8):
        copy_b(k).wait()
    corr_own[...] = jnp.concatenate([recv_b[0:64, 0:64], recv_b[64:128, 0:64]], axis=1).astype(bf16)

    @pl.when(y == 0)
    def _():
        corr_c[x] = corr_own[...]
        for k in range(1, 4):
            corr_column(k, 0).start()
        for k in range(1, 4):
            corr_column(k, 1).start()

    @pl.when(core == 0)
    def _():
        for k in range(1, 8):
            corr_row(k).start()
        corr_r[z] = corr_own[...]

    steps(7, 8)

    def bin_rows(f, i, at):
        binned_v[2 * f + i, at] = (data_v[2 * f + i, at].astype(f32) + added(i, at)).astype(bf16)

    build_rows(jnp.transpose(recv_b[...]), 512)
    build_cols(recv_b[...].astype(bf16), 1)
    for first, last in ((0, 64), (64, 256)):
        for i in range(2):
            for v in range(2):
                bin_rows(1, i, slice(256 * v + first, 256 * v + last))

        @pl.when(y == 0)
        def _():
            for v in range(2):
                at = slice(256 * v + first, 256 * v + last)
                cbuf[x, 2:4, at] = binned_v[2:4, at]

        @pl.when(core == 0)
        def _():
            rbuf[z, 2:4, first:last] = binned_v[2:4, first:last]

        if first == 0:
            steps(8, 9)
    steps(9, 10)
    build_cols(recv_b[...].astype(bf16), 0)
    bin_rows(0, 0, slice(0, 512))
    steps(10, 11)

    @pl.when(y != 0)
    def _():
        corr_arrived(x)
        for k in range(1, 4):
            corr_column(k, 1).start()

    bin_rows(0, 1, slice(0, 512))
    steps(11, 12)

    for p in range(4):
        @pl.when((core != 0) | (z != p))
        def _():
            pltpu.make_async_remote_copy(
                src_ref=corr_own, dst_ref=corr_r.at[p], send_sem=cr_send.at[0], recv_sem=cr_recv.at[p],
                device_id=(lax.rem(r + 1, 8), s), device_id_type=MESH,
            ).wait_recv()

    def correct_rows(t):
        p = t - 12
        got = unpack(corr_r[p])
        build_rows(jnp.transpose(got.astype(f32)), 256)
        build_cols(got, 0)
        for i in range(2):
            rbuf_0[p, i] = (rbuf[p, i].astype(f32) + added(i, slice(0, 256))).astype(bf16)

    def correct_columns(t):
        p, i = (t - 16) // 2, lax.rem(t, 2)

        @pl.when(i == 0)
        def _():
            @pl.when(x != p)
            def _():
                corr_arrived(p)

            got = unpack(corr_c[p])
            build_rows(jnp.transpose(got.astype(f32)), 512)
            build_cols(got, 0)

        delta[p, i] = added(i, slice(0, 512))

    steps(12, 16, correct_rows)
    steps(16, 24, correct_columns)

    factor = 2048**-0.5

    def product(f, c_re, c_im):
        rows = c_re[0].shape[0]
        re = jnp.zeros((rows, 256), f32)
        im = jnp.zeros((rows, 256), f32)
        for p in range(4):
            r_re, r_im = (rbuf_0[p, 0], rbuf_0[p, 1]) if f == 0 else (rbuf[p, 2], rbuf[p, 3])
            re = re + jnp.dot(c_re[p], r_re, preferred_element_type=f32)
            re = re - jnp.dot(c_im[p], r_im, preferred_element_type=f32)
            im = im + jnp.dot(c_re[p], r_im, preferred_element_type=f32)
            im = im + jnp.dot(c_im[p], r_re, preferred_element_type=f32)
        return re * factor, im * factor

    def multiply(t):
        at = pl.ds(pl.multiple_of((t - 24) * 128, 128), 128)
        c_re, c_im = [
            [(cbuf[p, i, at].astype(f32) + delta[p, i, at]).astype(bf16) for p in range(4)] for i in range(2)
        ]
        out_v[0, at], out_v[1, at] = product(0, c_re, c_im)
        ats = [pl.ds(pl.multiple_of(256 * v + (t - 24) * 64, 64), 64) for v in range(2)]
        c_re, c_im = [
            [jnp.concatenate([cbuf[p, i, at] for at in ats], axis=0) for p in range(4)] for i in (2, 3)
        ]
        re, im = product(1, c_re, c_im)
        for v in range(2):
            out_v[2, ats[v]] = re[64 * v : 64 * (v + 1)]
            out_v[3, ats[v]] = im[64 * v : 64 * (v + 1)]

    steps(24, 28, multiply)

    for row in range(4):
        @pl.when(y == row)
        def _():
            for dx, v, p in streams:
                half = cbuf.at[p, :, pl.ds(v * 256, 256)]
                for way in TREE.get((dx, row), ()):
                    pltpu.make_async_remote_copy(
                        src_ref=half, dst_ref=half, send_sem=c_send.at[2 * dx + v, way_index[way]],
                        recv_sem=c_recv.at[2 * p + v, 0], device_id=target(way, v), device_id_type=MESH,
                    ).wait_send()

    def row_wait(p, ref, way):
        pltpu.make_async_remote_copy(
            src_ref=ref, dst_ref=ref, send_sem=r_send.at[p, way], recv_sem=r_recv.at[p, 0],
            device_id=(z_up, z_down, z_core)[way], device_id_type=MESH,
        ).wait_send()

    @pl.when(core == 0)
    def _():
        for dz, p in enumerate(row_panels):
            row_wait(p, rbuf.at[p], 2)
            if dz == 0:
                row_wait(p, rbuf.at[p], 0)
                row_wait(p, rbuf.at[p], 1)
            elif dz == 1:
                row_wait(p, rbuf.at[p, pl.ds(0, 2)], 0)
            elif dz == 3:
                row_wait(p, rbuf.at[p, pl.ds(2, 2)], 1)

    @pl.when(y == 0)
    def _():
        for k in range(1, 4):
            corr_column(k, 0).wait_send()

    for k in range(1, 4):
        corr_column(k, 1).wait_send()

    @pl.when(core == 0)
    def _():
        for k in range(1, 8):
            corr_row(k).wait_send()


def body(data, traces, weight, dest, bins):
    f32, bf16 = jnp.float32, jnp.bfloat16
    dma = pltpu.SemaphoreType.DMA
    return pl.pallas_call(
        kernel,
        out_shape=(
            pltpu.VMEM((4, 512, 256), bf16),
            pltpu.VMEM((4, 512, 256), f32),
        ),
        in_specs=[pl.BlockSpec(memory_space=pltpu.HBM)] * 6,
        out_specs=(pl.BlockSpec(memory_space=pltpu.VMEM),) * 2,
        scratch_shapes=[
            pltpu.VMEM((8, 128), f32),
            pltpu.VMEM((1, 512), f32),
            pltpu.VMEM((1, 512), jnp.int32),
            pltpu.VMEM((1, 512), jnp.int32),
            pltpu.VMEM((512, 2048), f32),
            pltpu.VMEM((4, 512, 256), bf16),
            pltpu.VMEM((128, 128), f32),
            pltpu.VMEM((128, 128), f32),
            pltpu.VMEM((128, 128), f32),
            pltpu.VMEM((128, 128), f32),
            pltpu.VMEM((512, 1024), bf16),
            pltpu.VMEM((4, 1024, 256), bf16),
            pltpu.VMEM((4, 4, 512, 256), bf16),
            pltpu.VMEM((4, 4, 256, 256), bf16),
            pltpu.VMEM((4, 2, 256, 256), bf16),
            pltpu.VMEM((4, 64, 128), bf16),
            pltpu.VMEM((4, 64, 128), bf16),
            pltpu.VMEM((64, 128), bf16),
            pltpu.VMEM((4, 2, 512, 256), f32),
            dma((9,)),
            dma((15,)),
            dma((15,)),
            dma((7,)),
            dma((7,)),
            dma((8, 4)),
            dma((8, CHUNKS)),
            dma((4, 3)),
            dma((4, 8)),
            dma((6,)),
            dma((4,)),
            dma((7,)),
            dma((4,)),
        ],
        compiler_params=pltpu.CompilerParams(
            collective_id=0, has_side_effects=True, vmem_limit_bytes=40 * 2**20
        ),
        cost_estimate=pl.CostEstimate(flops=5 * 10**9, bytes_accessed=9 * 2**20, transcendentals=0),
    )(
        *(
            pltpu.with_memory_space_constraint(one, pltpu.HBM)
            for one in (
                jnp.asarray(table_t()),
                weight.reshape(1, 512),
                dest.reshape(1, 512),
                bins.reshape(1, 512),
                data,
                traces,
            )
        )
    )


def solution(mesh):
    placed = (
        P(None, "rcv", "shot"),
        P(("rcv", "shot"), None),
        P(("rcv", "shot")),
        P(("rcv", "shot"), None),
        P(("rcv", "shot")),
    )
    return jax.shard_map(
        body,
        mesh=mesh,
        in_specs=placed,
        out_specs=(P(None, "rcv", "shot"), P(None, "rcv", "shot")),
        check_vma=False,
    )
```

```python
import functools
import math

import jax
import jax.numpy as jnp
import numpy as np
from jax import lax
from jax.experimental import pallas as pl
from jax.experimental.pallas import tpu as pltpu
from jax.sharding import PartitionSpec as P

MESH = pl.DeviceIdType.MESH
FAR_SHOT = (10, 9, 11, 6, 7, 5, 14, 13, 15, 8, 2, 3, 1, 4, 12)
FAR_RCV = (4, 5, 3, 2, 6, 7, 1)
SLOTS = 8
PERIOD = 128
CHUNKS = 16
ROWS_LATE = 9
STRETCH = 3

TREE = {
    (0, 0): ("b", "+y", "-y"),
    (3, 0): ("b",),
    (0, 1): ("f", "+y"),
    (1, 1): ("f", "-y"),
    (0, 3): ("b",),
    (3, 3): ("b",),
    (2, 3): ("-y",),
    (0, 2): ("f", "b"),
    (1, 2): ("+y",),
    (3, 2): ("-y",),
}
STEP = {"f": (1, 0), "b": (3, 0), "+y": (0, 1), "-y": (0, 3)}


def tree_depths():
    depths, front = {(0, 0): 0}, [(0, 0)]
    while front:
        at = front.pop(0)
        for way in TREE.get(at, ()):
            to = ((at[0] + STEP[way][0]) % 4, (at[1] + STEP[way][1]) % 4)
            assert to not in depths
            depths[to] = depths[at] + 1
            front.append(to)
    assert len(depths) == 16
    return depths


DEPTHS = tree_depths()


def table_t():
    n = np.arange(PERIOD)
    rows = []
    for freq in (128, 256):
        angle = (freq * n % 2048) * (2.0 * math.pi / 2048)
        rows += [np.cos(angle), -np.sin(angle)]
    rows = np.stack(rows) * 2048**-0.5
    return np.concatenate([rows, np.zeros((4, PERIOD))]).astype(np.float32)


def kernel(
    table_hbm, weight_hbm, dest_hbm, bins_hbm, data_hbm, traces_hbm, binned_v, out_v,
    table, weight, dest, bins, traces_v, data_v, send_a, recv_a, send_b, recv_b, rows_1h, cols_1h,
    cbuf, rbuf, rbuf_0, corr_c, corr_r, corr_own, delta,
    in_sem, a_send, a_recv, b_send, b_recv, c_send, c_recv, r_send, r_recv,
    cc_send, cc_recv, cr_send, cr_recv,
):
    r = lax.axis_index("rcv")
    s = lax.axis_index("shot")
    x, y = s // 4, s % 4
    z, core = r // 2, r % 2
    f32, bf16 = jnp.float32, jnp.bfloat16

    barrier = pltpu.get_barrier_semaphore()
    for k in FAR_SHOT:
        pl.semaphore_signal(barrier, inc=1, device_id=(r, lax.rem(s + k, 16)), device_id_type=MESH)
    for k in FAR_RCV:
        pl.semaphore_signal(barrier, inc=1, device_id=(lax.rem(r + k, 8), s), device_id_type=MESH)

    small_in = [
        pltpu.make_async_copy(one, to, in_sem.at[5 + i])
        for i, (one, to) in enumerate(((dest_hbm, dest), (table_hbm, table), (weight_hbm, weight), (bins_hbm, bins)))
    ]
    trace_in = [
        pltpu.make_async_copy(traces_hbm.at[pl.ds(128 * i, 128)], traces_v.at[pl.ds(128 * i, 128)], in_sem.at[i])
        for i in range(4)
    ]
    data_in = pltpu.make_async_copy(data_hbm, data_v, in_sem.at[4])
    for one in small_in:
        one.start()
    for one in trace_in:
        one.start()
    data_in.start()

    for one in small_in:
        one.wait()
    owner = dest[...]
    owner = (owner & 15) * 8 + (owner >> 4)
    owner_1h = jnp.where(lax.broadcasted_iota(jnp.int32, (128, 512), 0) == owner, 1.0, 0.0)
    before = jnp.where(
        lax.broadcasted_iota(jnp.int32, (512, 512), 0) < lax.broadcasted_iota(jnp.int32, (512, 512), 1), 1.0, 0.0
    ).astype(bf16)
    owner_1h_b = owner_1h.astype(bf16)
    earlier = jnp.dot(owner_1h_b, before, preferred_element_type=f32)
    slot = jnp.sum(owner_1h * earlier, axis=0, keepdims=True)
    in_slot = lax.broadcasted_iota(jnp.int32, (SLOTS, 512), 0).astype(f32) == slot

    spectra = []
    for i in range(4):
        trace_in[i].wait()
        folded = traces_v[pl.ds(128 * i, 128), 0:PERIOD]
        for b in range(1, 16):
            folded = folded + traces_v[pl.ds(128 * i, 128), PERIOD * b : PERIOD * (b + 1)]
        spectra.append(
            lax.dot_general(
                table[...], folded, (((1,), (1,)), ((), ())),
                precision=lax.Precision.HIGHEST, preferred_element_type=f32,
            )
        )
    spectra = jnp.concatenate(spectra, axis=1)[0:4] * weight[...]
    high = spectra.astype(bf16).astype(f32)
    low = (spectra - high).astype(bf16).astype(f32)
    place = bins[...]
    words = [high[0:1], high[1:2], low[0:1], low[1:2]]
    words += [(place >> 16).astype(f32), ((place >> 8) & 255).astype(f32), (place & 255).astype(f32)]
    words += [jnp.zeros_like(weight[...]), high[2:3], high[3:4], low[2:3], low[3:4]]
    listing = [jnp.where(in_slot, word, 0.0) for word in words]
    listing.append(jnp.zeros((128 - SLOTS * len(words), 512), f32))
    listing = jnp.concatenate(listing, axis=0).astype(bf16)
    send_a[...] = lax.dot_general(owner_1h_b, listing, (((1,), (1,)), ((), ())), preferred_element_type=f32)

    data_in.wait()

    @pl.when(y == 0)
    def _():
        cbuf[x, 0:2] = data_v[0:2]

    @pl.when(core == 0)
    def _():
        rbuf[z, 0:2] = data_v[0:2, 0:256]

    streams = [(dx, v, lax.rem(x + (4 - dx if v == 0 else dx), 4)) for dx in range(4) for v in range(2)]
    up, down = lax.rem(x + 1, 4), lax.rem(x + 3, 4)

    def target(way, v):
        if way == "+y":
            return (r, x * 4 + lax.rem(y + 1, 4))
        if way == "-y":
            return (r, x * 4 + lax.rem(y + 3, 4))
        return (r, (up if (way == "f") == (v == 0) else down) * 4 + y)

    way_index = {way: i for i, way in enumerate(STEP)}

    def column_copy(dx, v, p, j, way):
        comp = (j // 8) * 2 + lax.rem(j, 2)
        start = v * 256 + lax.rem(j // 2, 4) * 64
        ref = cbuf.at[p, comp, pl.ds(pl.multiple_of(start, 64), 64)]
        return pltpu.make_async_remote_copy(
            src_ref=ref, dst_ref=ref, send_sem=c_send.at[2 * dx + v, way_index[way]],
            recv_sem=c_recv.at[2 * p + v, j], device_id=target(way, v), device_id_type=MESH,
        )

    z_up = (lax.rem(z + 1, 4) * 2 + core, s)
    z_down = (lax.rem(z + 3, 4) * 2 + core, s)
    z_core = (z * 2 + 1 - core, s)

    def row_copy(p, k, way):
        ref = rbuf.at[p, k // 2, pl.ds(pl.multiple_of(lax.rem(k, 2) * 128, 128), 128)]
        return pltpu.make_async_remote_copy(
            src_ref=ref, dst_ref=ref, send_sem=r_send.at[p, way], recv_sem=r_recv.at[p, k],
            device_id=(z_up, z_down, z_core)[way], device_id_type=MESH,
        )

    row_panels = [lax.rem(z + 4 - dz, 4) for dz in range(4)]

    def within(t, low, high, first, last, act):
        if low <= first and last <= high:
            act()
        elif first < high and low < last:
            pl.when((t >= low) & (t < high))(act)

    def step(t, first, last):
        for row in range(4):
            @pl.when(y == row)
            def _():
                for dx, v, p in streams:
                    delay = DEPTHS[dx, row] * STRETCH

                    def pass_on():
                        if delay:
                            column_copy(dx, v, p, t - delay, "f").wait_recv()
                        for way in TREE.get((dx, row), ()):
                            column_copy(dx, v, p, t - delay, way).start()

                    within(t, delay, delay + CHUNKS, first, last, pass_on)

        for side in range(2):
            @pl.when(core == side)
            def _():
                for dz, p in enumerate(row_panels):
                    delay = (min(dz, 4 - dz) + side) * STRETCH
                    for begin, k_first in ((0, 0), (0, 1), (0, 2), (0, 3), (ROWS_LATE, 4)):
                        def pass_on():
                            k = t - delay - begin + k_first
                            if begin == 0:
                                k = jnp.int32(k_first)
                            if delay:
                                row_copy(p, k, 0).wait_recv()
                            if side == 0:
                                row_copy(p, k, 2).start()
                                if dz == 0:
                                    row_copy(p, k, 0).start()
                                    row_copy(p, k, 1).start()
                                elif dz == 1:
                                    pl.when(lax.rem(k, 2) == 0)(lambda: row_copy(p, k, 0).start())
                                elif dz == 3:
                                    pl.when(lax.rem(k, 2) == 1)(lambda: row_copy(p, k, 1).start())

                        if begin:
                            within(t, delay + begin, delay + begin + 4, first, last, pass_on)
                        else:
                            at = delay + k_first // 2
                            within(t, at, at + 1, first, last, pass_on)

    def steps(first, last, work=None):
        if last == first + 1:
            step(first, first, last)
            if work:
                work(first)
            return

        @pl.loop(first, last)
        def _(t):
            step(t, first, last)
            if work:
                work(t)

    def copy_a(k):
        to = lax.rem(s + k, 16)
        return pltpu.make_async_remote_copy(
            src_ref=send_a.at[pl.ds(to * 8, 8)], dst_ref=recv_a.at[pl.ds(s * 8, 8)],
            send_sem=a_send.at[k - 1], recv_sem=a_recv.at[k - 1],
            device_id=(r, to), device_id_type=MESH,
        )

    def copy_b(k):
        to = lax.rem(r + k, 8)
        return pltpu.make_async_remote_copy(
            src_ref=send_b.at[pl.ds(to * 16, 16)], dst_ref=recv_b.at[pl.ds(r * 16, 16)],
            send_sem=b_send.at[k - 1], recv_sem=b_recv.at[k - 1],
            device_id=(to, s), device_id_type=MESH,
        )

    def corr_column(k, along_x):
        to = lax.rem(x + k, 4) * 4 + y if along_x else x * 4 + lax.rem(y + k, 4)
        return pltpu.make_async_remote_copy(
            src_ref=corr_c.at[x], dst_ref=corr_c.at[x], send_sem=cc_send.at[k - 1 + 3 * along_x],
            recv_sem=cc_recv.at[x], device_id=(r, to), device_id_type=MESH,
        )

    def corr_arrived(p):
        pltpu.make_async_remote_copy(
            src_ref=corr_own, dst_ref=corr_c.at[p], send_sem=cc_send.at[0], recv_sem=cc_recv.at[p],
            device_id=(r, lax.rem(s + 1, 16)), device_id_type=MESH,
        ).wait_recv()

    def unpack(packed):
        return jnp.concatenate([packed[:, 0:64], packed[:, 64:128]], axis=0)

    def corr_row(k):
        return pltpu.make_async_remote_copy(
            src_ref=corr_own, dst_ref=corr_r.at[z], send_sem=cr_send.at[k - 1], recv_sem=cr_recv.at[z],
            device_id=(lax.rem(r + k, 8), s), device_id_type=MESH,
        )

    def build_rows(got_t, count):
        for slot_at in range(SLOTS):
            high_row = got_t[32 + slot_at : 33 + slot_at]
            low_row = got_t[40 + slot_at : 41 + slot_at]
            for h in range(count // 256):
                row = jnp.where(high_row == float(h), low_row, -1.0).astype(bf16)
                rows_1h[256 * h : 256 * (h + 1), 128 * slot_at : 128 * (slot_at + 1)] = jnp.where(
                    iota_row == row, jnp.bfloat16(1), jnp.bfloat16(0)
                )

    def build_cols(got, f):
        for slot_at in range(SLOTS):
            column = got[:, 48 + slot_at : 49 + slot_at]
            at_column = iota_col == column
            for i, w in enumerate(range(8 * f, 8 * f + 4)):
                value = got[:, 8 * w + slot_at : 8 * w + slot_at + 1]
                cols_1h[i, 128 * slot_at : 128 * (slot_at + 1)] = jnp.where(at_column, value, jnp.bfloat16(0))

    def added(i, at):
        total = jnp.dot(rows_1h[at], cols_1h[i], preferred_element_type=f32)
        return total + jnp.dot(rows_1h[at], cols_1h[i + 2], preferred_element_type=f32)

    iota_row = lax.broadcasted_iota(jnp.int32, (256, 128), 0).astype(f32).astype(bf16)
    iota_col = lax.broadcasted_iota(jnp.int32, (128, 256), 1).astype(f32).astype(bf16)

    pl.semaphore_wait(barrier, 22)

    for k in FAR_SHOT:
        copy_a(k).start()
    own = pl.ds(pl.multiple_of(s * 8, 8), 8)
    recv_a[own] = send_a[own]
    steps(0, 3)
    for k in range(1, 16):
        copy_a(k).wait()
    for k in range(8):
        send_b[16 * k : 16 * (k + 1)] = recv_a[pl.ds(k, 16, stride=8)]
    for k in FAR_RCV:
        copy_b(k).start()
    own = pl.ds(pl.multiple_of(r * 16, 16), 16)
    recv_b[own] = send_b[own]
    steps(3, 6)
    for k in range(1, 8):
        copy_b(k).wait()
    corr_own[...] = jnp.concatenate([recv_b[0:64, 0:64], recv_b[64:128, 0:64]], axis=1).astype(bf16)

    @pl.when(y == 0)
    def _():
        corr_c[x] = corr_own[...]
        for k in range(1, 4):
            corr_column(k, 0).start()
        for k in range(1, 4):
            corr_column(k, 1).start()

    @pl.when(core == 0)
    def _():
        for k in range(1, 8):
            corr_row(k).start()
        corr_r[z] = corr_own[...]

    steps(6, 7)

    def bin_rows(f, i, at):
        binned_v[2 * f + i, at] = (data_v[2 * f + i, at].astype(f32) + added(i, at)).astype(bf16)

    build_rows(jnp.transpose(recv_b[...]), 512)
    build_cols(recv_b[...].astype(bf16), 1)
    for first, last in ((0, 64), (64, 256)):
        for i in range(2):
            for v in range(2):
                bin_rows(1, i, slice(256 * v + first, 256 * v + last))

        @pl.when(y == 0)
        def _():
            for v in range(2):
                at = slice(256 * v + first, 256 * v + last)
                cbuf[x, 2:4, at] = binned_v[2:4, at]

        @pl.when(core == 0)
        def _():
            rbuf[z, 2:4, first:last] = binned_v[2:4, first:last]

        if first == 0:
            steps(7, 9)
    steps(9, 10)
    build_cols(recv_b[...].astype(bf16), 0)
    for i in range(2):
        bin_rows(0, i, slice(0, 512))

    for p in range(4):
        @pl.when((core != 0) | (z != p))
        def _():
            pltpu.make_async_remote_copy(
                src_ref=corr_own, dst_ref=corr_r.at[p], send_sem=cr_send.at[0], recv_sem=cr_recv.at[p],
                device_id=(lax.rem(r + 1, 8), s), device_id_type=MESH,
            ).wait_recv()

    def correct_rows(t):
        p = t - 10
        got = unpack(corr_r[p])
        build_rows(jnp.transpose(got.astype(f32)), 256)
        build_cols(got, 0)
        for i in range(2):
            rbuf_0[p, i] = (rbuf[p, i].astype(f32) + added(i, slice(0, 256))).astype(bf16)

    def correct_columns(t):
        p, i = (t - 14) // 2, lax.rem(t, 2)

        @pl.when(i == 0)
        def _():
            @pl.when(x != p)
            def _():
                corr_arrived(p)

            got = unpack(corr_c[p])
            build_rows(jnp.transpose(got.astype(f32)), 512)
            build_cols(got, 0)

        delta[p, i] = added(i, slice(0, 512))

    steps(10, 11, correct_rows)

    @pl.when(y != 0)
    def _():
        corr_arrived(x)
        for k in range(1, 4):
            corr_column(k, 1).start()

    steps(11, 14, correct_rows)
    steps(14, 22, correct_columns)

    factor = 2048**-0.5

    def product(f, c_re, c_im):
        rows = c_re[0].shape[0]
        re = jnp.zeros((rows, 256), f32)
        im = jnp.zeros((rows, 256), f32)
        for p in range(4):
            r_re, r_im = (rbuf_0[p, 0], rbuf_0[p, 1]) if f == 0 else (rbuf[p, 2], rbuf[p, 3])
            re = re + jnp.dot(c_re[p], r_re, preferred_element_type=f32)
            re = re - jnp.dot(c_im[p], r_im, preferred_element_type=f32)
            im = im + jnp.dot(c_re[p], r_im, preferred_element_type=f32)
            im = im + jnp.dot(c_im[p], r_re, preferred_element_type=f32)
        return re * factor, im * factor

    def multiply_0(t):
        at = pl.ds(pl.multiple_of((t - 22) * 128, 128), 128)
        c_re, c_im = [
            [(cbuf[p, i, at].astype(f32) + delta[p, i, at]).astype(bf16) for p in range(4)] for i in range(2)
        ]
        out_v[0, at], out_v[1, at] = product(0, c_re, c_im)

    def multiply_1(t):
        ats = [pl.ds(pl.multiple_of(256 * v + (t - 24) * 64, 64), 64) for v in range(2)]
        c_re, c_im = [
            [jnp.concatenate([cbuf[p, i, at] for at in ats], axis=0) for p in range(4)] for i in (2, 3)
        ]
        re, im = product(1, c_re, c_im)
        for v in range(2):
            out_v[2, ats[v]] = re[64 * v : 64 * (v + 1)]
            out_v[3, ats[v]] = im[64 * v : 64 * (v + 1)]

    def multiply_both(t):
        multiply_0(t)
        multiply_1(t)

    steps(22, 24, multiply_0)
    steps(24, 26, multiply_both)
    steps(26, 28, multiply_1)

    for row in range(4):
        @pl.when(y == row)
        def _():
            for dx, v, p in streams:
                half = cbuf.at[p, :, pl.ds(v * 256, 256)]
                for way in TREE.get((dx, row), ()):
                    pltpu.make_async_remote_copy(
                        src_ref=half, dst_ref=half, send_sem=c_send.at[2 * dx + v, way_index[way]],
                        recv_sem=c_recv.at[2 * p + v, 0], device_id=target(way, v), device_id_type=MESH,
                    ).wait_send()

    def row_wait(p, ref, way):
        pltpu.make_async_remote_copy(
            src_ref=ref, dst_ref=ref, send_sem=r_send.at[p, way], recv_sem=r_recv.at[p, 0],
            device_id=(z_up, z_down, z_core)[way], device_id_type=MESH,
        ).wait_send()

    @pl.when(core == 0)
    def _():
        for dz, p in enumerate(row_panels):
            row_wait(p, rbuf.at[p], 2)
            if dz == 0:
                row_wait(p, rbuf.at[p], 0)
                row_wait(p, rbuf.at[p], 1)
            elif dz == 1:
                row_wait(p, rbuf.at[p, pl.ds(0, 2)], 0)
            elif dz == 3:
                row_wait(p, rbuf.at[p, pl.ds(2, 2)], 1)

    @pl.when(y == 0)
    def _():
        for k in range(1, 4):
            corr_column(k, 0).wait_send()

    for k in range(1, 4):
        corr_column(k, 1).wait_send()

    @pl.when(core == 0)
    def _():
        for k in range(1, 8):
            corr_row(k).wait_send()


def write_out(binned_v, out_v, binned_hbm, mult_hbm, sem):
    copies = [
        pltpu.make_async_copy(one.at[i], to.at[i], sem.at[n, i])
        for n, (one, to) in enumerate(((out_v, mult_hbm), (binned_v, binned_hbm)))
        for i in range(4)
    ]
    for one in copies:
        one.start()
    for one in copies:
        one.wait()


def body(data, traces, weight, dest, bins):
    f32, bf16 = jnp.float32, jnp.bfloat16
    dma = pltpu.SemaphoreType.DMA
    results = pl.pallas_call(
        kernel,
        out_shape=(
            pltpu.VMEM((4, 512, 256), bf16),
            pltpu.VMEM((4, 512, 256), f32),
        ),
        in_specs=[pl.BlockSpec(memory_space=pltpu.HBM)] * 6,
        out_specs=(pl.BlockSpec(memory_space=pltpu.VMEM),) * 2,
        scratch_shapes=[
            pltpu.VMEM((8, 128), f32),
            pltpu.VMEM((1, 512), f32),
            pltpu.VMEM((1, 512), jnp.int32),
            pltpu.VMEM((1, 512), jnp.int32),
            pltpu.VMEM((512, 2048), f32),
            pltpu.VMEM((4, 512, 256), bf16),
            pltpu.VMEM((128, 128), f32),
            pltpu.VMEM((128, 128), f32),
            pltpu.VMEM((128, 128), f32),
            pltpu.VMEM((128, 128), f32),
            pltpu.VMEM((512, 1024), bf16),
            pltpu.VMEM((4, 1024, 256), bf16),
            pltpu.VMEM((4, 4, 512, 256), bf16),
            pltpu.VMEM((4, 4, 256, 256), bf16),
            pltpu.VMEM((4, 2, 256, 256), bf16),
            pltpu.VMEM((4, 64, 128), bf16),
            pltpu.VMEM((4, 64, 128), bf16),
            pltpu.VMEM((64, 128), bf16),
            pltpu.VMEM((4, 2, 512, 256), f32),
            dma((9,)),
            dma((15,)),
            dma((15,)),
            dma((7,)),
            dma((7,)),
            dma((8, 4)),
            dma((8, CHUNKS)),
            dma((4, 3)),
            dma((4, 8)),
            dma((6,)),
            dma((4,)),
            dma((7,)),
            dma((4,)),
        ],
        compiler_params=pltpu.CompilerParams(
            collective_id=0, has_side_effects=True, vmem_limit_bytes=40 * 2**20
        ),
        cost_estimate=pl.CostEstimate(flops=5 * 10**9, bytes_accessed=9 * 2**20, transcendentals=0),
    )(
        *(
            pltpu.with_memory_space_constraint(one, pltpu.HBM)
            for one in (
                jnp.asarray(table_t()),
                weight.reshape(1, 512),
                dest.reshape(1, 512),
                bins.reshape(1, 512),
                data,
                traces,
            )
        )
    )
    return pl.pallas_call(
        write_out,
        out_shape=(
            jax.ShapeDtypeStruct((4, 512, 256), bf16),
            jax.ShapeDtypeStruct((4, 512, 256), f32),
        ),
        in_specs=[pl.BlockSpec(memory_space=pltpu.VMEM)] * 2,
        out_specs=(pl.BlockSpec(memory_space=pltpu.HBM),) * 2,
        scratch_shapes=[dma((2, 4))],
        cost_estimate=pl.CostEstimate(flops=0, bytes_accessed=3 * 2**20, transcendentals=0),
    )(*(pltpu.with_memory_space_constraint(one, pltpu.VMEM) for one in results))


def solution(mesh):
    placed = (
        P(None, "rcv", "shot"),
        P(("rcv", "shot"), None),
        P(("rcv", "shot")),
        P(("rcv", "shot"), None),
        P(("rcv", "shot")),
    )
    return jax.shard_map(
        body,
        mesh=mesh,
        in_specs=placed,
        out_specs=(P(None, "rcv", "shot"), P(None, "rcv", "shot")),
        check_vma=False,
    )
```

```python
import functools
import math

import jax
import jax.numpy as jnp
import numpy as np
from jax import lax
from jax.experimental import pallas as pl
from jax.experimental.pallas import tpu as pltpu
from jax.sharding import PartitionSpec as P

MESH = pl.DeviceIdType.MESH
FAR_SHOT = (10, 9, 11, 6, 7, 5, 14, 13, 15, 8, 2, 3, 1, 4, 12)
FAR_RCV = (4, 5, 3, 2, 6, 7, 1)
SLOTS = 8
PERIOD = 128
CHUNKS = 16
ROWS_LATE = 9
STRETCH = 3

TREE = {
    (0, 0): ("b", "+y", "-y"),
    (3, 0): ("b",),
    (0, 1): ("f", "+y"),
    (1, 1): ("f", "-y"),
    (0, 3): ("b",),
    (3, 3): ("b",),
    (2, 3): ("-y",),
    (0, 2): ("f", "b"),
    (1, 2): ("+y",),
    (3, 2): ("-y",),
}
STEP = {"f": (1, 0), "b": (3, 0), "+y": (0, 1), "-y": (0, 3)}


def tree_depths():
    depths, front = {(0, 0): 0}, [(0, 0)]
    while front:
        at = front.pop(0)
        for way in TREE.get(at, ()):
            to = ((at[0] + STEP[way][0]) % 4, (at[1] + STEP[way][1]) % 4)
            assert to not in depths
            depths[to] = depths[at] + 1
            front.append(to)
    assert len(depths) == 16
    return depths


DEPTHS = tree_depths()


def table_t():
    n = np.arange(PERIOD)
    rows = []
    for freq in (128, 256):
        angle = (freq * n % 2048) * (2.0 * math.pi / 2048)
        rows += [np.cos(angle), -np.sin(angle)]
    rows = np.stack(rows) * 2048**-0.5
    return np.concatenate([rows, np.zeros((4, PERIOD))]).astype(np.float32)


def kernel(
    table_hbm, weight_hbm, dest_hbm, bins_hbm, data_hbm, traces_hbm, binned_v, out_v,
    table, weight, dest, bins, traces_v, data_v, send_a, recv_a, send_b, recv_b, rows_1h, cols_1h,
    cbuf, rbuf, rbuf_0, corr_c, corr_r, corr_own, delta,
    in_sem, a_send, a_recv, b_send, b_recv, c_send, c_recv, r_send, r_recv,
    cc_send, cc_recv, cr_send, cr_recv,
):
    r = lax.axis_index("rcv")
    s = lax.axis_index("shot")
    x, y = s // 4, s % 4
    z, core = r // 2, r % 2
    f32, bf16 = jnp.float32, jnp.bfloat16

    barrier = pltpu.get_barrier_semaphore()
    for k in FAR_SHOT:
        pl.semaphore_signal(barrier, inc=1, device_id=(r, lax.rem(s + k, 16)), device_id_type=MESH)
    for k in FAR_RCV:
        pl.semaphore_signal(barrier, inc=1, device_id=(lax.rem(r + k, 8), s), device_id_type=MESH)

    small_in = [
        pltpu.make_async_copy(one, to, in_sem.at[5 + i])
        for i, (one, to) in enumerate(((dest_hbm, dest), (table_hbm, table), (weight_hbm, weight), (bins_hbm, bins)))
    ]
    trace_in = [
        pltpu.make_async_copy(traces_hbm.at[pl.ds(128 * i, 128)], traces_v.at[pl.ds(128 * i, 128)], in_sem.at[i])
        for i in range(4)
    ]
    data_in = pltpu.make_async_copy(data_hbm, data_v, in_sem.at[4])
    for one in small_in:
        one.start()
    for one in trace_in:
        one.start()
    data_in.start()

    for one in small_in:
        one.wait()
    owner = dest[...]
    owner = (owner & 15) * 8 + (owner >> 4)
    owner_1h = jnp.where(lax.broadcasted_iota(jnp.int32, (128, 512), 0) == owner, 1.0, 0.0)
    before = jnp.where(
        lax.broadcasted_iota(jnp.int32, (512, 512), 0) < lax.broadcasted_iota(jnp.int32, (512, 512), 1), 1.0, 0.0
    ).astype(bf16)
    owner_1h_b = owner_1h.astype(bf16)
    earlier = jnp.dot(owner_1h_b, before, preferred_element_type=f32)
    slot = jnp.sum(owner_1h * earlier, axis=0, keepdims=True)
    in_slot = lax.broadcasted_iota(jnp.int32, (SLOTS, 512), 0).astype(f32) == slot

    spectra = []
    for i in range(4):
        trace_in[i].wait()
        folded = traces_v[pl.ds(128 * i, 128), 0:PERIOD]
        for b in range(1, 16):
            folded = folded + traces_v[pl.ds(128 * i, 128), PERIOD * b : PERIOD * (b + 1)]
        spectra.append(
            lax.dot_general(
                table[...], folded, (((1,), (1,)), ((), ())),
                precision=lax.Precision.HIGHEST, preferred_element_type=f32,
            )
        )
    spectra = jnp.concatenate(spectra, axis=1)[0:4] * weight[...]
    high = spectra.astype(bf16).astype(f32)
    low = (spectra - high).astype(bf16).astype(f32)
    place = bins[...]
    words = [high[0:1], high[1:2], low[0:1], low[1:2]]
    words += [(place >> 16).astype(f32), ((place >> 8) & 255).astype(f32), (place & 255).astype(f32)]
    words += [jnp.zeros_like(weight[...]), high[2:3], high[3:4], low[2:3], low[3:4]]
    listing = [jnp.where(in_slot, word, 0.0) for word in words]
    listing.append(jnp.zeros((128 - SLOTS * len(words), 512), f32))
    listing = jnp.concatenate(listing, axis=0).astype(bf16)
    send_a[...] = lax.dot_general(owner_1h_b, listing, (((1,), (1,)), ((), ())), preferred_element_type=f32)

    data_in.wait()

    @pl.when(y == 0)
    def _():
        cbuf[x, 0:2] = data_v[0:2]

    @pl.when(core == 0)
    def _():
        rbuf[z, 0:2] = data_v[0:2, 0:256]

    streams = [(dx, v, lax.rem(x + (4 - dx if v == 0 else dx), 4)) for dx in range(4) for v in range(2)]
    up, down = lax.rem(x + 1, 4), lax.rem(x + 3, 4)

    def target(way, v):
        if way == "+y":
            return (r, x * 4 + lax.rem(y + 1, 4))
        if way == "-y":
            return (r, x * 4 + lax.rem(y + 3, 4))
        return (r, (up if (way == "f") == (v == 0) else down) * 4 + y)

    way_index = {way: i for i, way in enumerate(STEP)}

    def column_copy(dx, v, p, j, way):
        comp = (j // 8) * 2 + lax.rem(j, 2)
        start = v * 256 + lax.rem(j // 2, 4) * 64
        ref = cbuf.at[p, comp, pl.ds(pl.multiple_of(start, 64), 64)]
        return pltpu.make_async_remote_copy(
            src_ref=ref, dst_ref=ref, send_sem=c_send.at[2 * dx + v, way_index[way]],
            recv_sem=c_recv.at[2 * p + v, j], device_id=target(way, v), device_id_type=MESH,
        )

    z_up = (lax.rem(z + 1, 4) * 2 + core, s)
    z_down = (lax.rem(z + 3, 4) * 2 + core, s)
    z_core = (z * 2 + 1 - core, s)

    def row_copy(p, k, way):
        ref = rbuf.at[p, k // 2, pl.ds(pl.multiple_of(lax.rem(k, 2) * 128, 128), 128)]
        return pltpu.make_async_remote_copy(
            src_ref=ref, dst_ref=ref, send_sem=r_send.at[p, way], recv_sem=r_recv.at[p, k],
            device_id=(z_up, z_down, z_core)[way], device_id_type=MESH,
        )

    row_panels = [lax.rem(z + 4 - dz, 4) for dz in range(4)]

    def within(t, low, high, first, last, act):
        if low <= first and last <= high:
            act()
        elif first < high and low < last:
            pl.when((t >= low) & (t < high))(act)

    def step(t, first, last):
        for row in range(4):
            @pl.when(y == row)
            def _():
                for dx, v, p in streams:
                    delay = DEPTHS[dx, row] * STRETCH

                    def pass_on():
                        if delay:
                            column_copy(dx, v, p, t - delay, "f").wait_recv()
                        for way in TREE.get((dx, row), ()):
                            column_copy(dx, v, p, t - delay, way).start()

                    within(t, delay, delay + CHUNKS, first, last, pass_on)

        for side in range(2):
            @pl.when(core == side)
            def _():
                for dz, p in enumerate(row_panels):
                    delay = (min(dz, 4 - dz) + side) * STRETCH
                    for begin, k_first in ((0, 0), (0, 1), (0, 2), (0, 3), (ROWS_LATE, 4)):
                        def pass_on():
                            k = t - delay - begin + k_first
                            if begin == 0:
                                k = jnp.int32(k_first)
                            if delay:
                                row_copy(p, k, 0).wait_recv()
                            if side == 0:
                                row_copy(p, k, 2).start()
                                if dz == 0:
                                    row_copy(p, k, 0).start()
                                    row_copy(p, k, 1).start()
                                elif dz == 1:
                                    pl.when(lax.rem(k, 2) == 0)(lambda: row_copy(p, k, 0).start())
                                elif dz == 3:
                                    pl.when(lax.rem(k, 2) == 1)(lambda: row_copy(p, k, 1).start())

                        if begin:
                            within(t, delay + begin, delay + begin + 4, first, last, pass_on)
                        else:
                            at = delay + k_first // 2
                            within(t, at, at + 1, first, last, pass_on)

    def copy_a(k):
        to = lax.rem(s + k, 16)
        return pltpu.make_async_remote_copy(
            src_ref=send_a.at[pl.ds(to * 8, 8)], dst_ref=recv_a.at[pl.ds(s * 8, 8)],
            send_sem=a_send.at[k - 1], recv_sem=a_recv.at[k - 1],
            device_id=(r, to), device_id_type=MESH,
        )

    def copy_b(k):
        to = lax.rem(r + k, 8)
        return pltpu.make_async_remote_copy(
            src_ref=send_b.at[pl.ds(to * 16, 16)], dst_ref=recv_b.at[pl.ds(r * 16, 16)],
            send_sem=b_send.at[k - 1], recv_sem=b_recv.at[k - 1],
            device_id=(to, s), device_id_type=MESH,
        )

    def corr_column(k, along_x):
        to = lax.rem(x + k, 4) * 4 + y if along_x else x * 4 + lax.rem(y + k, 4)
        return pltpu.make_async_remote_copy(
            src_ref=corr_c.at[x], dst_ref=corr_c.at[x], send_sem=cc_send.at[k - 1 + 3 * along_x],
            recv_sem=cc_recv.at[x], device_id=(r, to), device_id_type=MESH,
        )

    def corr_arrived(p):
        pltpu.make_async_remote_copy(
            src_ref=corr_own, dst_ref=corr_c.at[p], send_sem=cc_send.at[0], recv_sem=cc_recv.at[p],
            device_id=(r, lax.rem(s + 1, 16)), device_id_type=MESH,
        ).wait_recv()

    def unpack(packed):
        return jnp.concatenate([packed[:, 0:64], packed[:, 64:128]], axis=0)

    def corr_row(k):
        return pltpu.make_async_remote_copy(
            src_ref=corr_own, dst_ref=corr_r.at[z], send_sem=cr_send.at[k - 1], recv_sem=cr_recv.at[z],
            device_id=(lax.rem(r + k, 8), s), device_id_type=MESH,
        )

    def build_rows(got_t, count):
        for slot_at in range(SLOTS):
            high_row = got_t[32 + slot_at : 33 + slot_at]
            low_row = got_t[40 + slot_at : 41 + slot_at]
            for h in range(count // 256):
                row = jnp.where(high_row == float(h), low_row, -1.0).astype(bf16)
                rows_1h[256 * h : 256 * (h + 1), 128 * slot_at : 128 * (slot_at + 1)] = jnp.where(
                    iota_row == row, jnp.bfloat16(1), jnp.bfloat16(0)
                )

    def build_cols(got, f):
        for slot_at in range(SLOTS):
            column = got[:, 48 + slot_at : 49 + slot_at]
            at_column = iota_col == column
            for i, w in enumerate(range(8 * f, 8 * f + 4)):
                value = got[:, 8 * w + slot_at : 8 * w + slot_at + 1]
                cols_1h[i, 128 * slot_at : 128 * (slot_at + 1)] = jnp.where(at_column, value, jnp.bfloat16(0))

    def added(i, at):
        total = jnp.dot(rows_1h[at], cols_1h[i], preferred_element_type=f32)
        return total + jnp.dot(rows_1h[at], cols_1h[i + 2], preferred_element_type=f32)

    iota_row = lax.broadcasted_iota(jnp.int32, (256, 128), 0).astype(f32).astype(bf16)
    iota_col = lax.broadcasted_iota(jnp.int32, (128, 256), 1).astype(f32).astype(bf16)

    pl.semaphore_wait(barrier, 22)

    for k in FAR_SHOT:
        copy_a(k).start()
    own = pl.ds(pl.multiple_of(s * 8, 8), 8)
    recv_a[own] = send_a[own]
    def bin_rows(f, i, at):
        binned_v[2 * f + i, at] = (data_v[2 * f + i, at].astype(f32) + added(i, at)).astype(bf16)

    def bin_second(first, last):
        for i in range(2):
            for v in range(2):
                bin_rows(1, i, slice(256 * v + first, 256 * v + last))

        @pl.when(y == 0)
        def _():
            for v in range(2):
                at = slice(256 * v + first, 256 * v + last)
                cbuf[x, 2:4, at] = binned_v[2:4, at]

        @pl.when(core == 0)
        def _():
            rbuf[z, 2:4, first:last] = binned_v[2:4, first:last]

    def exchange_over_rcv():
        for k in range(1, 16):
            copy_a(k).wait()
        for k in range(8):
            send_b[16 * k : 16 * (k + 1)] = recv_a[pl.ds(k, 16, stride=8)]
        for k in FAR_RCV:
            copy_b(k).start()
        own = pl.ds(pl.multiple_of(r * 16, 16), 16)
        recv_b[own] = send_b[own]

    def send_corrections():
        for k in range(1, 8):
            copy_b(k).wait()
        corr_own[...] = jnp.concatenate([recv_b[0:64, 0:64], recv_b[64:128, 0:64]], axis=1).astype(bf16)

        @pl.when(y == 0)
        def _():
            corr_c[x] = corr_own[...]
            for k in range(1, 4):
                corr_column(k, 0).start()
            for k in range(1, 4):
                corr_column(k, 1).start()

        @pl.when(core == 0)
        def _():
            for k in range(1, 8):
                corr_row(k).start()
            corr_r[z] = corr_own[...]

    def bin_first_rows():
        build_rows(jnp.transpose(recv_b[...]), 512)
        build_cols(recv_b[...].astype(bf16), 1)
        bin_second(0, 64)

    def bin_first():
        build_cols(recv_b[...].astype(bf16), 0)
        for i in range(2):
            bin_rows(0, i, slice(0, 512))

        for p in range(4):
            @pl.when((core != 0) | (z != p))
            def _():
                pltpu.make_async_remote_copy(
                    src_ref=corr_own, dst_ref=corr_r.at[p], send_sem=cr_send.at[0], recv_sem=cr_recv.at[p],
                    device_id=(lax.rem(r + 1, 8), s), device_id_type=MESH,
                ).wait_recv()

    def relay_corrections():
        @pl.when(y != 0)
        def _():
            corr_arrived(x)
            for k in range(1, 4):
                corr_column(k, 1).start()

    def correct_rows(t):
        p = t - 10
        got = unpack(corr_r[p])
        build_rows(jnp.transpose(got.astype(f32)), 256)
        build_cols(got, 0)
        for i in range(2):
            rbuf_0[p, i] = (rbuf[p, i].astype(f32) + added(i, slice(0, 256))).astype(bf16)

    def correct_columns(t):
        p, i = (t - 14) // 2, lax.rem(t, 2)

        @pl.when(i == 0)
        def _():
            @pl.when(x != p)
            def _():
                corr_arrived(p)

            got = unpack(corr_c[p])
            build_rows(jnp.transpose(got.astype(f32)), 512)
            build_cols(got, 0)

        delta[p, i] = added(i, slice(0, 512))

    factor = 2048**-0.5

    def product(f, c_re, c_im):
        rows = c_re[0].shape[0]
        re = jnp.zeros((rows, 256), f32)
        im = jnp.zeros((rows, 256), f32)
        for p in range(4):
            r_re, r_im = (rbuf_0[p, 0], rbuf_0[p, 1]) if f == 0 else (rbuf[p, 2], rbuf[p, 3])
            re = re + jnp.dot(c_re[p], r_re, preferred_element_type=f32)
            re = re - jnp.dot(c_im[p], r_im, preferred_element_type=f32)
            im = im + jnp.dot(c_re[p], r_im, preferred_element_type=f32)
            im = im + jnp.dot(c_im[p], r_re, preferred_element_type=f32)
        return re * factor, im * factor

    def multiply_0(t):
        at = pl.ds(pl.multiple_of((t - 22) * 128, 128), 128)
        c_re, c_im = [
            [(cbuf[p, i, at].astype(f32) + delta[p, i, at]).astype(bf16) for p in range(4)] for i in range(2)
        ]
        out_v[0, at], out_v[1, at] = product(0, c_re, c_im)

    def multiply_1(t):
        ats = [pl.ds(pl.multiple_of(256 * v + (t - 24) * 64, 64), 64) for v in range(2)]
        c_re, c_im = [
            [jnp.concatenate([cbuf[p, i, at] for at in ats], axis=0) for p in range(4)] for i in (2, 3)
        ]
        re, im = product(1, c_re, c_im)
        for v in range(2):
            out_v[2, ats[v]] = re[64 * v : 64 * (v + 1)]
            out_v[3, ats[v]] = im[64 * v : 64 * (v + 1)]

    once = {
        2: exchange_over_rcv, 5: send_corrections, 6: bin_first_rows, 8: lambda: bin_second(64, 256),
        9: bin_first, 10: relay_corrections,
    }

    @pl.loop(0, 28)
    def _(t):
        step(t, 0, 28)
        for turn, work in once.items():
            pl.when(t == turn)(work)
        for first, last, work in (
            (10, 14, correct_rows), (14, 22, correct_columns), (22, 26, multiply_0), (24, 28, multiply_1)
        ):
            pl.when((t >= first) & (t < last))(functools.partial(work, t))

    for row in range(4):
        @pl.when(y == row)
        def _():
            for dx, v, p in streams:
                half = cbuf.at[p, :, pl.ds(v * 256, 256)]
                for way in TREE.get((dx, row), ()):
                    pltpu.make_async_remote_copy(
                        src_ref=half, dst_ref=half, send_sem=c_send.at[2 * dx + v, way_index[way]],
                        recv_sem=c_recv.at[2 * p + v, 0], device_id=target(way, v), device_id_type=MESH,
                    ).wait_send()

    def row_wait(p, ref, way):
        pltpu.make_async_remote_copy(
            src_ref=ref, dst_ref=ref, send_sem=r_send.at[p, way], recv_sem=r_recv.at[p, 0],
            device_id=(z_up, z_down, z_core)[way], device_id_type=MESH,
        ).wait_send()

    @pl.when(core == 0)
    def _():
        for dz, p in enumerate(row_panels):
            row_wait(p, rbuf.at[p], 2)
            if dz == 0:
                row_wait(p, rbuf.at[p], 0)
                row_wait(p, rbuf.at[p], 1)
            elif dz == 1:
                row_wait(p, rbuf.at[p, pl.ds(0, 2)], 0)
            elif dz == 3:
                row_wait(p, rbuf.at[p, pl.ds(2, 2)], 1)

    @pl.when(y == 0)
    def _():
        for k in range(1, 4):
            corr_column(k, 0).wait_send()

    for k in range(1, 4):
        corr_column(k, 1).wait_send()

    @pl.when(core == 0)
    def _():
        for k in range(1, 8):
            corr_row(k).wait_send()


def write_out(binned_v, out_v, binned_hbm, mult_hbm, sem):
    copies = [
        pltpu.make_async_copy(one.at[i], to.at[i], sem.at[n, i])
        for n, (one, to) in enumerate(((out_v, mult_hbm), (binned_v, binned_hbm)))
        for i in range(4)
    ]
    for one in copies:
        one.start()
    for one in copies:
        one.wait()


def body(data, traces, weight, dest, bins):
    f32, bf16 = jnp.float32, jnp.bfloat16
    dma = pltpu.SemaphoreType.DMA
    results = pl.pallas_call(
        kernel,
        out_shape=(
            pltpu.VMEM((4, 512, 256), bf16),
            pltpu.VMEM((4, 512, 256), f32),
        ),
        in_specs=[pl.BlockSpec(memory_space=pltpu.HBM)] * 6,
        out_specs=(pl.BlockSpec(memory_space=pltpu.VMEM),) * 2,
        scratch_shapes=[
            pltpu.VMEM((8, 128), f32),
            pltpu.VMEM((1, 512), f32),
            pltpu.VMEM((1, 512), jnp.int32),
            pltpu.VMEM((1, 512), jnp.int32),
            pltpu.VMEM((512, 2048), f32),
            pltpu.VMEM((4, 512, 256), bf16),
            pltpu.VMEM((128, 128), f32),
            pltpu.VMEM((128, 128), f32),
            pltpu.VMEM((128, 128), f32),
            pltpu.VMEM((128, 128), f32),
            pltpu.VMEM((512, 1024), bf16),
            pltpu.VMEM((4, 1024, 256), bf16),
            pltpu.VMEM((4, 4, 512, 256), bf16),
            pltpu.VMEM((4, 4, 256, 256), bf16),
            pltpu.VMEM((4, 2, 256, 256), bf16),
            pltpu.VMEM((4, 64, 128), bf16),
            pltpu.VMEM((4, 64, 128), bf16),
            pltpu.VMEM((64, 128), bf16),
            pltpu.VMEM((4, 2, 512, 256), f32),
            dma((9,)),
            dma((15,)),
            dma((15,)),
            dma((7,)),
            dma((7,)),
            dma((8, 4)),
            dma((8, CHUNKS)),
            dma((4, 3)),
            dma((4, 8)),
            dma((6,)),
            dma((4,)),
            dma((7,)),
            dma((4,)),
        ],
        compiler_params=pltpu.CompilerParams(
            collective_id=0, has_side_effects=True, vmem_limit_bytes=40 * 2**20
        ),
        cost_estimate=pl.CostEstimate(flops=5 * 10**9, bytes_accessed=9 * 2**20, transcendentals=0),
    )(
        *(
            pltpu.with_memory_space_constraint(one, pltpu.HBM)
            for one in (
                jnp.asarray(table_t()),
                weight.reshape(1, 512),
                dest.reshape(1, 512),
                bins.reshape(1, 512),
                data,
                traces,
            )
        )
    )
    return pl.pallas_call(
        write_out,
        out_shape=(
            jax.ShapeDtypeStruct((4, 512, 256), bf16),
            jax.ShapeDtypeStruct((4, 512, 256), f32),
        ),
        in_specs=[pl.BlockSpec(memory_space=pltpu.VMEM)] * 2,
        out_specs=(pl.BlockSpec(memory_space=pltpu.HBM),) * 2,
        scratch_shapes=[dma((2, 4))],
        cost_estimate=pl.CostEstimate(flops=0, bytes_accessed=3 * 2**20, transcendentals=0),
    )(*(pltpu.with_memory_space_constraint(one, pltpu.VMEM) for one in results))


def solution(mesh):
    placed = (
        P(None, "rcv", "shot"),
        P(("rcv", "shot"), None),
        P(("rcv", "shot")),
        P(("rcv", "shot"), None),
        P(("rcv", "shot")),
    )
    return jax.shard_map(
        body,
        mesh=mesh,
        in_specs=placed,
        out_specs=(P(None, "rcv", "shot"), P(None, "rcv", "shot")),
        check_vma=False,
    )
```
